128 devices in a mesh: section: 8 (over y, core), dp: 8 (over z_hi, x), tensor: 2 (over z_lo).
Axes of the slice: x: 4, y: 4, z: 4 (z_hi: 2, z_lo: 2; z = z_hi * 2 + z_lo), core: 2. Of those that a mesh axis runs over, the one named last changes fastest.
Arguments:
- states_in: bfloat16 [2, 8, 128, 3584], P(None, 'section', ('dp', 'tensor')), may hold values from -40 to 40
- entering: bfloat16 [1, 2, 128, 3584], P(None, None, ('dp', 'tensor')), may hold values from -40 to 40
- saved: bfloat16 [2, 2, 8, 128, 3584], P(None, None, 'section', ('dp', 'tensor')), may hold values from -40 to 40
- cotangent: bfloat16 [2, 8, 128, 3584], P(None, 'section', ('dp', 'tensor')), may hold values from -1.5 to 1.5
- cot_entering: bfloat16 [1, 2, 128, 3584], P(None, None, ('dp', 'tensor')), may hold values from -1.5 to 1.5
- gains: bfloat16 [8, 3584], replicated, may hold values from 0.5 to 1.5
- up_rows: bfloat16 [8, 2, 9216, 3584], P('section', None, ('dp', 'tensor')), may hold values from -1 to 1, as said below
- down_rows: bfloat16 [8, 2, 9216, 3584], P('section', None, ('dp', 'tensor')), may hold values from -1 to 1, as said below
Outputs:
- states_out: bfloat16 [2, 2, 8, 128, 3584], P(None, None, 'section', ('dp', 'tensor'))
- input_grads: bfloat16 [2, 2, 8, 128, 3584], P(None, None, 'section', ('dp', 'tensor'))
- grad_up: bfloat16 [8, 9216, 3584], P('section', ('dp', 'tensor'))
- grad_down: bfloat16 [8, 9216, 3584], P('section', ('dp', 'tensor'))
The draws below stay inside these ranges and needn't reach their ends.
Inputs may be any that keep to these rules, and one draw needn't show every extreme that they name: up_rows[s, 1] equals up_rows[7 - s, 0] for every section s: both slots hold copies of a layer. down_rows[s, 1] equals down_rows[7 - s, 0] for every section s: both slots hold copies of a layer.
All inputs are finite; a program needn't handle non-finite values.
Results may differ from the reference program's by a relative error of at most 0.007.
Values may be sent and summed in bfloat16 or wider, within the bound.
A program may use at most 128 MiB of HBM per device.

```python
import math
import jax
import jax.numpy as jnp
from jax import lax

D = 3584
FF = 9216
STEPS = 2
SECTIONS = 8
TOKENS = 128


def scales(key, extent, lowest, highest):
    row_key, column_key = jax.random.split(key)
    row_scale = jnp.exp(jax.random.uniform(row_key, extent[:-1] + (1,), jnp.float32, math.log(lowest), math.log(highest)))
    column_scale = jnp.exp(jax.random.uniform(column_key, (extent[-1],), jnp.float32, math.log(lowest), math.log(highest)))
    return row_scale * column_scale


def rough_base(key, extent, bound):
    return jnp.clip(jax.random.normal(key, extent, jnp.float32), -bound, bound)


def draw_states_in(key, part):
    key = jax.random.fold_in(key, 1)
    base_key, scale_key = jax.random.split(key, 2)
    extent = (2, SECTIONS, TOKENS, D)
    base = rough_base(base_key, extent, 4.0)
    return (base * scales(scale_key, extent, 0.3, 3.0)).astype(jnp.bfloat16)


def draw_entering(key, part):
    key = jax.random.fold_in(key, 2)
    base_key, scale_key = jax.random.split(key, 2)
    extent = (STEPS - 1, 2, TOKENS, D)
    base = rough_base(base_key, extent, 4.0)
    return (base * scales(scale_key, extent, 0.3, 3.0)).astype(jnp.bfloat16)


def draw_saved(key, part):
    key = jax.random.fold_in(key, 3)
    base_key, scale_key = jax.random.split(key, 2)
    extent = (STEPS, 2, SECTIONS, TOKENS, D)
    base = rough_base(base_key, extent, 4.0)
    return (base * scales(scale_key, extent, 0.3, 3.0)).astype(jnp.bfloat16)


def draw_up_rows(key, part):
    key = jax.random.fold_in(key, 7)
    base = rough_base(key, (SECTIONS, FF, D), 4.0) * D ** (-0.5)
    return jnp.stack([base, jnp.flip(base, 0)], axis=1).astype(jnp.bfloat16)


def draw_down_rows(key, part):
    key = jax.random.fold_in(key, 9)
    base = rough_base(key, (SECTIONS, FF, D), 4.0) * FF ** (-0.5)
    return jnp.stack([base, jnp.flip(base, 0)], axis=1).astype(jnp.bfloat16)


def levels(rng, shape, shards, least, top_value):
    def one(dim, blocks):
        heights = jax.random.uniform(jax.random.fold_in(jax.random.fold_in(rng, 6), dim), (blocks,), jnp.float32, least / len(shards), top_value / len(shards))
        return jnp.repeat(jnp.exp(heights), shape[dim] // blocks).reshape((-1,) + (1,) * (len(shape) - dim - 1))

    level = one(*shards[0])
    for cut in shards[1:]:
        level = level * one(*cut)
    return level


def centred(key, dims, scale, limit, shards=(), dtype=jnp.bfloat16):
    drawn = scale * jax.random.normal(key, dims, jnp.float32)
    if shards:
        drawn = drawn * levels(key, dims, shards, -0.22, 0.18)
    return jnp.clip(drawn, -limit, limit).astype(dtype)


def setup_inputs(seed: int = 0) -> dict:
    key_list = jax.random.split(jax.random.key(seed), 9)
    return {
        "states_in": draw_states_in(jax.random.fold_in(key_list[8], 71), 0),
        "entering": draw_entering(jax.random.fold_in(key_list[8], 71), 0),
        "saved": draw_saved(jax.random.fold_in(key_list[8], 71), 0),
        "cotangent": centred(key_list[3], (2, SECTIONS, TOKENS, D), 0.25, 1.5, ((1, 8), (2, 16))),
        "cot_entering": centred(key_list[4], (STEPS - 1, 2, TOKENS, D), 0.25, 1.5, ((2, 16),)),
        "gains": jnp.clip(jax.random.uniform(key_list[5], (SECTIONS, D), jnp.float32, 0.5, 1.5), 0.5, 1.5).astype(jnp.bfloat16),
        "up_rows": draw_up_rows(jax.random.fold_in(key_list[8], 71), 0),
        "down_rows": draw_down_rows(jax.random.fold_in(key_list[8], 71), 0),
    }


EPSILON = 1e-06

def contract_last(former, latter):
    return lax.dot_general(former, latter, (((1,), (1,)), ((), ())), preferred_element_type=jnp.float32)

def contract_first(former, latter):
    return lax.dot_general(former, latter, (((0,), (0,)), ((), ())), preferred_element_type=jnp.float32)

def normalize(states, scaling):
    widened = states.astype(jnp.float32)
    factor = lax.rsqrt(lax.optimization_barrier(jnp.mean(widened * widened, axis=-1, keepdims=True)) + EPSILON)
    normed = (widened * factor * scaling).astype(jnp.bfloat16)
    return (widened, factor, normed)

def norm_back(widened, factor, scaling, upstream, d_normed):
    scaled = d_normed * scaling
    unit_rows = widened * factor
    d_norm = factor * (scaled - unit_rows * lax.optimization_barrier(jnp.mean(unit_rows * scaled, axis=-1, keepdims=True)))
    return (upstream.astype(jnp.float32) + d_norm).astype(jnp.bfloat16)

def layer_forward(states, scaling, up_rows, down_rows):
    widened, factor, normed = normalize(states, scaling)
    activated = jax.nn.silu(contract_last(normed, up_rows)).astype(jnp.bfloat16)
    branch = jnp.dot(activated, down_rows, preferred_element_type=jnp.float32)
    return (widened + branch).astype(jnp.bfloat16)

def layer_backward(saved_in, upstream, scaling, up_rows, down_rows):
    widened, factor, normed = normalize(saved_in, scaling)
    hidden = contract_last(normed, up_rows)
    activated = jax.nn.silu(hidden).astype(jnp.bfloat16)
    gating = jax.nn.sigmoid(hidden)
    d_hidden = (contract_last(upstream, down_rows) * gating * (1.0 + hidden * (1.0 - gating))).astype(jnp.bfloat16)
    d_normed = jnp.dot(d_hidden, up_rows, preferred_element_type=jnp.float32)
    d_states = norm_back(widened, factor, scaling, upstream, d_normed)
    return (d_states, (normed, upstream, activated, d_hidden))

def joined(operand_list):
    return tuple((jnp.concatenate(members, axis=0) for members in zip(*operand_list)))

def reference(states_in, entering, saved, cotangent, cot_entering, gains, up_rows, down_rows):
    sections = up_rows.shape[0]
    periods = saved.shape[0]
    gain_table = [[gains[station].astype(jnp.float32), gains[sections - 1 - station].astype(jnp.float32)] for station in range(sections)]
    inflow = [[states_in[course, station] for station in range(sections)] for course in range(2)]
    upstream = [[cotangent[course, station] for station in range(sections)] for course in range(2)]
    stored = [[[] for station in range(sections)] for course in range(2)]
    produced_all = []
    returned_all = []
    for period in range(periods):
        produced = [[layer_forward(inflow[course][station], gain_table[station][course], up_rows[station, course], down_rows[station, course]) for station in range(sections)] for course in range(2)]
        returned = [[], []]
        for course in range(2):
            for station in range(sections):
                d_states, operands = layer_backward(saved[period, course, station], upstream[course][station], gain_table[station][course], up_rows[station, course], down_rows[station, course])
                returned[course].append(d_states)
                stored[course][station].append(operands)
        produced_all.append(jnp.stack([jnp.stack(produced[course]) for course in range(2)]))
        returned_all.append(jnp.stack([jnp.stack(returned[course]) for course in range(2)]))
        if period + 1 < periods:
            inflow = [[entering[period, 0]] + produced[0][:-1], produced[1][1:] + [entering[period, 1]]]
            upstream = [returned[0][1:] + [cot_entering[period, 0]], [cot_entering[period, 1]] + returned[1][:-1]]
    grad_up = []
    grad_down = []
    for station in range(sections):
        near_terms = joined(stored[0][station])
        far_terms = joined(stored[1][sections - 1 - station])
        near_up = contract_first(near_terms[3], near_terms[0])
        near_down = contract_first(near_terms[2], near_terms[1])
        far_up = lax.optimization_barrier(contract_first(far_terms[3], far_terms[0]).astype(jnp.bfloat16)).astype(jnp.float32)
        far_down = lax.optimization_barrier(contract_first(far_terms[2], far_terms[1]).astype(jnp.bfloat16)).astype(jnp.float32)
        grad_up.append((near_up + far_up).astype(jnp.bfloat16))
        grad_down.append((near_down + far_down).astype(jnp.bfloat16))
    return (jnp.stack(produced_all), jnp.stack(returned_all), jnp.stack(grad_up), jnp.stack(grad_down))
```

```python
import jax
import jax.numpy as jnp
from jax import lax
from jax.sharding import PartitionSpec as P

EPSILON = 1e-06
GROUP = ("dp", "tensor")


def contract_last(former, latter):
    return lax.dot_general(
        former, latter, (((1,), (1,)), ((), ())), preferred_element_type=jnp.float32
    )


def contract_first(former, latter):
    return lax.dot_general(
        former, latter, (((0,), (0,)), ((), ())), preferred_element_type=jnp.float32
    )


def normalize(states, scaling):
    widened = states.astype(jnp.float32)
    factor = lax.rsqrt(jnp.mean(widened * widened, axis=-1, keepdims=True) + EPSILON)
    return widened, factor, (widened * factor * scaling).astype(jnp.bfloat16)


def norm_back(widened, factor, scaling, upstream, d_normed):
    scaled = d_normed * scaling
    unit_rows = widened * factor
    d_norm = factor * (scaled - unit_rows * jnp.mean(unit_rows * scaled, axis=-1, keepdims=True))
    return (upstream.astype(jnp.float32) + d_norm).astype(jnp.bfloat16)


def gather(block):
    return lax.all_gather(block, GROUP, axis=0, tiled=True)


def spread_sum(partial):
    count = lax.axis_size(GROUP)
    blocks = partial.astype(jnp.bfloat16)
    blocks = lax.all_to_all(blocks, GROUP, split_axis=0, concat_axis=0, tiled=True)
    return blocks.reshape((count, -1) + partial.shape[1:]).astype(jnp.float32).sum(0)


def body(states_in, entering, saved, cotangent, cot_entering, gains, up_rows, down_rows):
    sections = lax.axis_size("section")
    position = lax.axis_index("section")
    mirror = [(i, sections - 1 - i) for i in range(sections)]
    gain = lax.dynamic_index_in_dim(gains, position, 0, keepdims=True).astype(jnp.float32)
    up, down = up_rows[0, 0], down_rows[0, 0]
    periods = saved.shape[0]
    far = jnp.concatenate([states_in[1], cotangent[1]] + [saved[k, 1] for k in range(periods)], 0)
    far = lax.ppermute(far, "section", mirror)
    rows = jnp.concatenate([states_in[0, 0], far[0]], 0)
    grads = jnp.concatenate([cotangent[0, 0], far[1]], 0)
    stored = [jnp.concatenate([saved[k, 0, 0], far[2 + k]], 0) for k in range(periods)]
    produced_all, returned_all, terms = [], [], []
    for period in range(periods):
        wide, _, lead = normalize(rows, gain)
        wide_back, factor_back, trail = normalize(stored[period], gain)
        lead_all, trail_all, grads_all = gather(lead), gather(trail), gather(grads)
        acted = jax.nn.silu(contract_last(lead_all, up)).astype(jnp.bfloat16)
        hidden = contract_last(trail_all, up)
        gating = jax.nn.sigmoid(hidden)
        d_hidden = (
            contract_last(grads_all, down) * gating * (1.0 + hidden * (1.0 - gating))
        ).astype(jnp.bfloat16)
        acted_back = (hidden * gating).astype(jnp.bfloat16)
        terms.append((acted_back, grads_all, d_hidden, trail_all))
        out = jnp.dot(acted, down, preferred_element_type=jnp.float32)
        d_normed = jnp.dot(d_hidden, up, preferred_element_type=jnp.float32)
        produced = (wide + spread_sum(out)).astype(jnp.bfloat16)
        returned = norm_back(wide_back, factor_back, gain, grads, spread_sum(d_normed))
        produced_all.append(produced)
        returned_all.append(returned)
        if period + 1 < periods:
            onward = lax.ppermute(produced, "section", [(i, i + 1) for i in range(sections - 1)])
            back = lax.ppermute(returned, "section", [(i + 1, i) for i in range(sections - 1)])
            fresh = jnp.concatenate([entering[period, 0], entering[period, 1]], 0)
            fresh_back = jnp.concatenate([cot_entering[period, 0], cot_entering[period, 1]], 0)
            rows = jnp.where(position == 0, fresh, onward)
            grads = jnp.where(position == sections - 1, fresh_back, back)
    acted_back, grads_all, d_hidden, trail_all = (jnp.concatenate(m, 0) for m in zip(*terms))
    grad_up = contract_first(d_hidden, trail_all).astype(jnp.bfloat16)[None]
    grad_down = contract_first(acted_back, grads_all).astype(jnp.bfloat16)[None]
    half = produced_all[0].shape[0] // 2
    results = jnp.stack([jnp.stack(produced_all), jnp.stack(returned_all)])
    results_far = lax.ppermute(results[:, :, half:], "section", mirror)
    both = jnp.stack([results[:, :, :half], results_far], 2)[:, :, :, None]
    return both[0], both[1], grad_up, grad_down


def solution(mesh):
    group = ("dp", "tensor")
    placed = (
        P(None, "section", group, None),
        P(None, None, group, None),
        P(None, None, "section", group, None),
        P(None, "section", group, None),
        P(None, None, group, None),
        P(),
        P("section", None, group, None),
        P("section", None, group, None),
    )
    return jax.shard_map(
        body,
        mesh=mesh,
        in_specs=placed,
        out_specs=(
            P(None, None, "section", group, None),
            P(None, None, "section", group, None),
            P("section", group, None),
            P("section", group, None),
        ),
        check_vma=False,
    )
```

```python
import functools

import jax
import jax.numpy as jnp
from jax import lax
from jax.experimental import pallas as pl
from jax.experimental.pallas import tpu as pltpu
from jax.sharding import PartitionSpec as P

EPSILON = 1e-06
MESH = pl.DeviceIdType.MESH
F32, BF16 = jnp.float32, jnp.bfloat16
FA, NA, GA, NB, FB, GB = range(6)
RING = 4


def contract_last(former, latter):
    return lax.dot_general(former, latter, (((1,), (1,)), ((), ())), preferred_element_type=F32)


def mean(value):
    return jnp.mean(value, axis=-1, keepdims=True)


def kernel(
    states_in, entering, saved, cotangent, cot_entering, gains, up_rows, down_rows,
    states_out, input_grads, grad_up, grad_down,
    up, down, gathered, partial, pass_on, from_prev, from_next, summed, scattered,
    rows, grads, far_out, far_in, hop_out, hop_in, mirror_out, mirror_in,
    slopes, hidden_kept, active_kept, flipped, staged,
    load_sem, store_sem, ag_send, ag_recv, rs_send, rs_recv, far_send, far_recv,
    hop_send, hop_recv, mirror_send, mirror_recv,
):
    s = lax.axis_index("section")
    d = lax.axis_index("dp")
    t = lax.axis_index("tensor")
    sections = lax.axis_size("section")
    width = up.shape[-1]
    half = width // 2
    features = 2 * width
    units = up.shape[1]
    place = {"x": d % RING, "z": (d // RING) * 2 + t}

    def device(section, x, z):
        return (section, (z // 2) * RING + x, z % 2)

    def along(axis, step):
        moved = dict(place)
        moved[axis] = (place[axis] + step) % RING
        return device(s, moved["x"], moved["z"])

    mirror = device(sections - 1 - s, place["x"], place["z"])
    after = device((s + 1) % sections, place["x"], place["z"])
    before = device((s + sections - 1) % sections, place["x"], place["z"])

    loads = [
        pltpu.make_async_copy(
            source.at[0, 0, :, pl.ds(h * width, width)], target.at[h], load_sem.at[2 * n + h]
        )
        for n, (source, target) in enumerate(((up_rows, up), (down_rows, down)))
        for h in range(2)
    ]
    for load in loads:
        load.start()

    barrier = pltpu.get_barrier_semaphore()
    partners = [along(axis, step) for axis in "xz" for step in (1, 2, 3)] + [mirror, after, before]
    for partner in partners:
        pl.semaphore_signal(barrier, inc=1, device_id=partner, device_id_type=MESH)
    pl.semaphore_wait(barrier, len(partners))

    sends = []

    def send(source, target, send_sem, recv_sem, device_id):
        copy = pltpu.make_async_remote_copy(
            src_ref=source, dst_ref=target, send_sem=send_sem, recv_sem=recv_sem,
            device_id=device_id, device_id_type=MESH,
        )
        copy.start()
        sends.append(copy)

    def arrive(target, send_sem, recv_sem, device_id):
        pltpu.make_async_remote_copy(
            src_ref=target, dst_ref=target, send_sem=send_sem, recv_sem=recv_sem,
            device_id=device_id, device_id_type=MESH,
        ).wait_recv()

    inner, outer = ("x", "z"), ("z", "x")
    low, high, whole = pl.ds(0, half), pl.ds(half, half), pl.ds(0, width)

    def slab(ref, index, h, step, lanes):
        at = (place[outer[h]] + step) % RING
        return ref.at[index, h, at, :, :, lanes] if h == 0 else ref.at[index, h, :, at, :, lanes]

    def block(ref, index, h, step):
        at = dict(place)
        at[inner[h]] = (place[inner[h]] + step) % RING
        return ref.at[index, h, at["z"], at["x"]]

    def gather_inner(a):
        for h in range(2):
            for step in (1, 3, 2):
                own = block(gathered, a, h, 0)
                sems = (ag_send.at[a, h, step - 1], ag_recv.at[a, h, step - 1])
                send(own, own, *sems, along(inner[h], step))

    def gather_outer(a):
        for h in range(2):
            for step in (1, 2, 3):
                sems = (ag_send.at[a, h, step - 1], ag_recv.at[a, h, step - 1])
                arrive(block(gathered, a, h, -step), *sems, along(inner[h], step))
            own = slab(gathered, a, h, 0, whole)
            for n, step in ((3, 1), (4, -1)):
                send(own, own, ag_send.at[a, h, n], ag_recv.at[a, h, n], along(outer[h], step))

    def gather_relay(a):
        for h in range(2):
            for n, step, lanes in ((3, 1, low), (4, -1, high)):
                sems = (ag_send.at[a, h, n], ag_recv.at[a, h, n])
                arrive(slab(gathered, a, h, -step, whole), *sems, along(outer[h], step))
                sems = (ag_send.at[a, h, n + 2], ag_recv.at[a, h, n + 2])
                passed = slab(gathered, a, h, -step, lanes)
                send(passed, passed, *sems, along(outer[h], step))

    def gather_end(a):
        for h in range(2):
            for n, step, lanes in ((5, 1, low), (6, -1, high)):
                sems = (ag_send.at[a, h, n], ag_recv.at[a, h, n])
                arrive(slab(gathered, a, h, -2 * step, lanes), *sems, along(outer[h], step))

    def scatter_start(p, h):
        def put(n, step, lanes, target, to):
            send(
                slab(partial, p, h, step, lanes), target.at[p, h, :, :, lanes],
                rs_send.at[p, h, n], rs_recv.at[p, h, n], along(outer[h], to),
            )

        put(0, 2, low, pass_on, 1)
        put(1, 2, high, pass_on, -1)
        put(2, 1, high, from_prev, 1)
        put(3, -1, low, from_next, -1)

    def scatter_relay(p):
        for h in range(2):
            for n, step, lanes, target in ((0, 1, low, from_prev), (1, -1, high, from_next)):
                passing = pass_on.at[p, h, :, :, lanes]
                arrive(passing, rs_send.at[p, h, n], rs_recv.at[p, h, n], along(outer[h], step))
                mine = slab(partial, p, h, step, lanes)
                mine[...] = (mine[...].astype(F32) + passing[...].astype(F32)).astype(BF16)
                send(
                    mine, target.at[p, h, :, :, lanes],
                    rs_send.at[p, h, n + 4], rs_recv.at[p, h, n + 4], along(outer[h], step),
                )

    def scatter_inner(p):
        for h in range(2):
            for n, lanes, target, step in (
                (2, high, from_prev, 1), (3, low, from_next, -1), (4, low, from_prev, 1), (5, high, from_next, -1),
            ):
                landed = target.at[p, h, :, :, lanes]
                arrive(landed, rs_send.at[p, h, n], rs_recv.at[p, h, n], along(outer[h], step))
            total = slab(partial, p, h, 0, whole)[...].astype(F32)
            total = total + from_prev[p, h].astype(F32) + from_next[p, h].astype(F32)
            summed[p, h] = total.astype(BF16)
            for step in (1, 3, 2):
                at = (place[inner[h]] + step) % RING
                send(
                    summed.at[p, h, at], scattered.at[p, h, step - 1],
                    rs_send.at[p, h, 5 + step], rs_recv.at[p, h, 5 + step], along(inner[h], step),
                )

    def scatter_end(p):
        halves = []
        for h in range(2):
            total = summed[p, h, pl.ds(place[inner[h]], 1)][0].astype(F32)
            for step in (1, 2, 3):
                landed = scattered.at[p, h, step - 1]
                sems = (rs_send.at[p, h, 5 + step], rs_recv.at[p, h, 5 + step])
                arrive(landed, *sems, along(inner[h], step))
                total = total + landed[...].astype(F32)
            halves.append(total)
        return jnp.concatenate(halves, axis=1)

    def put_block(a, value):
        value = value.astype(BF16)
        for h in range(2):
            block(gathered, a, h, 0)[...] = value[:, h * width : (h + 1) * width]

    def factor_of(value):
        return lax.rsqrt(mean(value * value) + EPSILON)

    def normed(value):
        return value * factor_of(value) * gain

    def tokens(a, h):
        return gathered[a, h].reshape(RING * RING * 16, width)

    def onto_units(a, weights):
        return contract_last(tokens(a, 0), weights[0]) + contract_last(tokens(a, 1), weights[1])

    def onto_features(p, value, weights):
        tile = 256
        for h in range(2):
            def one(n, carry):
                lanes = pl.ds(pl.multiple_of(n * tile, tile), tile)
                product = jnp.dot(value, weights[h, :, lanes], preferred_element_type=F32)
                partial[p, h, :, :, :, lanes] = product.astype(BF16).reshape(RING, RING, 16, tile)
                return carry

            lax.fori_loop(0, width // tile, one, 0)
            scatter_start(p, h)

    def forward(p, a):
        hidden = onto_units(a, up)
        active = (hidden * jax.nn.sigmoid(hidden)).astype(BF16)
        onto_features(p, active, down)

    def backward_hidden(period, a):
        hidden = onto_units(a, up)
        gating = jax.nn.sigmoid(hidden)
        active_kept[...] = (hidden * gating).astype(BF16)
        hidden_kept[...] = gating * (1.0 + hidden * (1.0 - gating))
        flipped[1, period] = active_kept[...].T

    def backward(p, period, a):
        slopes[...] = (onto_units(a, down) * hidden_kept[...]).astype(BF16)
        onto_features(p, slopes[...], up)

    def backward_keep(period):
        flipped[0, period] = slopes[...].T

    def weight_grad(kind, h, target, first, second):
        tile = 256

        def one(n, carry):
            lanes = pl.ds(pl.multiple_of(n * tile, tile), tile)
            total = jnp.dot(
                flipped[kind, 0], gathered[first, h, :, :, :, lanes].reshape(-1, tile), preferred_element_type=F32
            ) + jnp.dot(
                flipped[kind, 1], gathered[second, h, :, :, :, lanes].reshape(-1, tile), preferred_element_type=F32
            )
            staged[kind, h, :, lanes] = total.astype(BF16)
            return carry

        lax.fori_loop(0, width // tile, one, 0)
        copy = pltpu.make_async_copy(
            staged.at[kind, h], target.at[0, :, pl.ds(h * width, width)], store_sem.at[kind, h]
        )
        copy.start()
        return copy

    def hop(n, value, to):
        hop_out[n] = value.astype(BF16)
        send(hop_out.at[n], hop_in.at[n], hop_send.at[n], hop_recv.at[n], to)

    def hopped(n, to):
        arrive(hop_in.at[n], hop_send.at[n], hop_recv.at[n], to)
        return hop_in[n].astype(F32)

    def deliver(n, target, period, value):
        value = value.astype(BF16)
        mirror_out[n] = value
        send(mirror_out.at[n], mirror_in.at[n], mirror_send.at[n], mirror_recv.at[n], mirror)
        target[period, 0, 0] = value.astype(F32)[:8].astype(BF16)

    def delivered(n, target, period):
        arrive(mirror_in.at[n], mirror_send.at[n], mirror_recv.at[n], mirror)
        target[period, 1, 0] = mirror_in[n].astype(F32)[8:].astype(BF16)

    def wide(value):
        return value.astype(F32)

    def joined(first, second):
        return jnp.concatenate([wide(first), wide(second)], axis=0)

    far_out[0] = joined(states_in[1, 0], cotangent[1, 0]).astype(BF16)
    send(far_out.at[0], far_in.at[0], far_send.at[0], far_recv.at[0], mirror)
    far_out[1] = joined(saved[0, 1, 0], saved[1, 1, 0]).astype(BF16)
    send(far_out.at[1], far_in.at[1], far_send.at[1], far_recv.at[1], mirror)

    chosen = lax.broadcasted_iota(jnp.int32, gains.shape, 0) == s
    gain = jnp.sum(jnp.where(chosen, wide(gains[...]), 0.0), axis=0, keepdims=True)

    arrive(far_in.at[0], far_send.at[0], far_recv.at[0], mirror)
    far = wide(far_in[0])
    rows[0] = jnp.concatenate([wide(states_in[0, 0]), far[:8]], axis=0)
    put_block(FA, normed(rows[0]))
    gather_inner(FA)
    grads[0] = jnp.concatenate([wide(cotangent[0, 0]), far[8:]], axis=0)
    put_block(GA, grads[0])
    arrive(far_in.at[1], far_send.at[1], far_recv.at[1], mirror)
    far = wide(far_in[1])
    rows[1] = jnp.concatenate([wide(saved[0, 0, 0]), far[:8]], axis=0)
    put_block(NA, normed(rows[1]))
    rows[2] = jnp.concatenate([wide(saved[1, 0, 0]), far[8:]], axis=0)
    put_block(NB, normed(rows[2]))
    gather_outer(FA)
    gather_inner(NA)
    gather_inner(GA)
    gather_relay(FA)
    gather_outer(NA)
    gather_end(FA)
    for load in loads:
        load.wait()
    forward(0, FA)
    gather_relay(NA)
    gather_outer(GA)
    scatter_relay(0)
    gather_end(NA)
    backward_hidden(0, NA)
    gather_relay(GA)
    gather_inner(NB)
    scatter_inner(0)
    gather_end(GA)
    backward(1, 0, GA)
    gather_outer(NB)
    produced = (rows[0] + scatter_end(0)).astype(BF16)
    hop(0, produced, after)
    deliver(0, states_out, 0, produced)
    backward_keep(0)
    gather_relay(NB)
    rows[3] = jnp.where(s == 0, joined(entering[0, 0], entering[0, 1]), hopped(0, after))
    put_block(FB, normed(rows[3]))
    gather_inner(FB)
    scatter_relay(1)
    gather_outer(FB)
    gather_end(NB)
    backward_hidden(1, NB)
    scatter_inner(1)
    gather_relay(FB)

    def returned(n, cot, p):
        scaled = scatter_end(p) * gain
        factor = factor_of(rows[n])
        unit = rows[n] * factor
        return (cot + factor * (scaled - unit * mean(unit * scaled))).astype(BF16)

    back = returned(1, grads[0], 1)
    hop(1, back, before)
    deliver(1, input_grads, 0, back)
    gather_end(FB)
    forward(2, FB)
    grads[1] = jnp.where(
        s == sections - 1, joined(cot_entering[0, 0], cot_entering[0, 1]), hopped(1, before)
    )
    put_block(GB, grads[1])
    gather_inner(GB)
    scatter_relay(2)
    gather_outer(GB)
    gather_relay(GB)
    scatter_inner(2)
    gather_end(GB)
    backward(3, 1, GB)
    produced = (rows[3] + scatter_end(2)).astype(BF16)
    deliver(2, states_out, 1, produced)
    stores = [weight_grad(1, 0, grad_down, GA, GB)]
    scatter_relay(3)
    stores.append(weight_grad(1, 1, grad_down, GA, GB))
    backward_keep(1)
    stores.append(weight_grad(0, 0, grad_up, NA, NB))
    scatter_inner(3)
    stores.append(weight_grad(0, 1, grad_up, NA, NB))
    back = returned(2, grads[1], 3)
    deliver(3, input_grads, 1, back)
    for n, target, period in (
        (0, states_out, 0), (1, input_grads, 0), (2, states_out, 1), (3, input_grads, 1),
    ):
        delivered(n, target, period)
    for copy in stores:
        copy.wait()
    for copy in sends:
        copy.wait_send()


def body(states_in, entering, saved, cotangent, cot_entering, gains, up_rows, down_rows):
    units, features = up_rows.shape[2:]
    width = features // 2
    dma, vmem = pltpu.SemaphoreType.DMA, pltpu.VMEM
    in_vmem = pl.BlockSpec(memory_space=pltpu.VMEM)
    anywhere = pl.BlockSpec(memory_space=pl.ANY)
    grid_rows = (RING, RING, 16, width)
    return pl.pallas_call(
        kernel,
        out_shape=(
            jax.ShapeDtypeStruct(saved.shape, BF16),
            jax.ShapeDtypeStruct(saved.shape, BF16),
            jax.ShapeDtypeStruct((1, units, features), BF16),
            jax.ShapeDtypeStruct((1, units, features), BF16),
        ),
        in_specs=[in_vmem] * 6 + [anywhere] * 2,
        out_specs=(in_vmem, in_vmem, anywhere, anywhere),
        scratch_shapes=[
            vmem((2, units, width), BF16),
            vmem((2, units, width), BF16),
            vmem((6, 2) + grid_rows, BF16),
            vmem((4, 2) + grid_rows, BF16),
            vmem((4, 2) + grid_rows[1:], BF16),
            vmem((4, 2) + grid_rows[1:], BF16),
            vmem((4, 2) + grid_rows[1:], BF16),
            vmem((4, 2) + grid_rows[1:], BF16),
            vmem((4, 2, 3, 16, width), BF16),
            vmem((4, 16, features), F32),
            vmem((2, 16, features), F32),
            vmem((2, 16, features), BF16),
            vmem((2, 16, features), BF16),
            vmem((2, 16, features), BF16),
            vmem((2, 16, features), BF16),
            vmem((4, 16, features), BF16),
            vmem((4, 16, features), BF16),
            vmem((256, units), BF16),
            vmem((256, units), F32),
            vmem((256, units), BF16),
            vmem((2, 2, units, 256), BF16),
            vmem((2, 2, units, width), BF16),
            dma((4,)),
            dma((2, 2)),
            dma((6, 2, 7)),
            dma((6, 2, 7)),
            dma((4, 2, 9)),
            dma((4, 2, 9)),
            dma((2,)),
            dma((2,)),
            dma((2,)),
            dma((2,)),
            dma((4,)),
            dma((4,)),
        ],
        compiler_params=pltpu.CompilerParams(
            collective_id=0, has_side_effects=True, vmem_limit_bytes=60 * 2**20
        ),
        cost_estimate=pl.CostEstimate(flops=15 * 10**9, bytes_accessed=17 * 10**6, transcendentals=0),
    )(states_in, entering, saved, cotangent, cot_entering, gains, up_rows, down_rows)


def solution(mesh):
    group = ("dp", "tensor")
    placed = (
        P(None, "section", group, None),
        P(None, None, group, None),
        P(None, None, "section", group, None),
        P(None, "section", group, None),
        P(None, None, group, None),
        P(),
        P("section", None, group, None),
        P("section", None, group, None),
    )
    return jax.shard_map(
        body,
        mesh=mesh,
        in_specs=placed,
        out_specs=(
            P(None, None, "section", group, None),
            P(None, None, "section", group, None),
            P("section", group, None),
            P("section", group, None),
        ),
        check_vma=False,
    )
```

```python
import functools

import jax
import jax.numpy as jnp
from jax import lax
from jax.experimental import pallas as pl
from jax.experimental.pallas import tpu as pltpu
from jax.sharding import PartitionSpec as P

EPSILON = 1e-06
MESH = pl.DeviceIdType.MESH
F32, BF16 = jnp.float32, jnp.bfloat16
FA, NA, GA, NB, FB, GB = range(6)
RING = 4


def contract_last(former, latter):
    return lax.dot_general(former, latter, (((1,), (1,)), ((), ())), preferred_element_type=F32)


def mean(value):
    return jnp.mean(value, axis=-1, keepdims=True)


def kernel(
    states_in, entering, saved, cotangent, cot_entering, gains, up_rows, down_rows,
    states_out, input_grads, grad_up, grad_down,
    up, down, gathered, partial, pass_on, from_prev, from_next, summed, scattered,
    rows, grads, far_out, far_in, hop_out, hop_in, mirror_out, mirror_in,
    slopes, hidden_kept, active_kept, flipped,
    load_sem, ag_send, ag_recv, rs_send, rs_recv, far_send, far_recv,
    hop_send, hop_recv, mirror_send, mirror_recv,
):
    s = lax.axis_index("section")
    d = lax.axis_index("dp")
    t = lax.axis_index("tensor")
    sections = lax.axis_size("section")
    width = up.shape[-1]
    half = width // 2
    features = 2 * width
    units = up.shape[1]
    place = {"x": d % RING, "z": (d // RING) * 2 + t}

    def device(section, x, z):
        return (section, (z // 2) * RING + x, z % 2)

    def along(axis, step):
        moved = dict(place)
        moved[axis] = (place[axis] + step) % RING
        return device(s, moved["x"], moved["z"])

    mirror = device(sections - 1 - s, place["x"], place["z"])
    after = device((s + 1) % sections, place["x"], place["z"])
    before = device((s + sections - 1) % sections, place["x"], place["z"])

    loads = [
        pltpu.make_async_copy(
            source.at[0, 0, :, pl.ds(h * width, width)], target.at[h], load_sem.at[2 * n + h]
        )
        for n, (source, target) in enumerate(((up_rows, up), (down_rows, down)))
        for h in range(2)
    ]
    for load in loads:
        load.start()

    barrier = pltpu.get_barrier_semaphore()
    partners = [along(axis, step) for axis in "xz" for step in (1, 2, 3)] + [mirror, after, before]
    for partner in partners:
        pl.semaphore_signal(barrier, inc=1, device_id=partner, device_id_type=MESH)
    pl.semaphore_wait(barrier, len(partners))

    sends = []

    def send(source, target, send_sem, recv_sem, device_id):
        copy = pltpu.make_async_remote_copy(
            src_ref=source, dst_ref=target, send_sem=send_sem, recv_sem=recv_sem,
            device_id=device_id, device_id_type=MESH,
        )
        copy.start()
        sends.append(copy)

    def arrive(target, send_sem, recv_sem, device_id):
        pltpu.make_async_remote_copy(
            src_ref=target, dst_ref=target, send_sem=send_sem, recv_sem=recv_sem,
            device_id=device_id, device_id_type=MESH,
        ).wait_recv()

    inner, outer = ("x", "z"), ("z", "x")
    low, high, whole = pl.ds(0, half), pl.ds(half, half), pl.ds(0, width)

    def slab(ref, index, h, step, lanes):
        at = (place[outer[h]] + step) % RING
        return ref.at[index, h, at, :, :, lanes] if h == 0 else ref.at[index, h, :, at, :, lanes]

    def block(ref, index, h, step):
        at = dict(place)
        at[inner[h]] = (place[inner[h]] + step) % RING
        return ref.at[index, h, at["z"], at["x"]]

    def gather_inner(a):
        for h in range(2):
            for step in (1, 3, 2):
                own = block(gathered, a, h, 0)
                sems = (ag_send.at[a, h, step - 1], ag_recv.at[a, h, step - 1])
                send(own, own, *sems, along(inner[h], step))

    def gather_outer(a):
        for h in range(2):
            for step in (1, 2, 3):
                sems = (ag_send.at[a, h, step - 1], ag_recv.at[a, h, step - 1])
                arrive(block(gathered, a, h, -step), *sems, along(inner[h], step))
            own = slab(gathered, a, h, 0, whole)
            for n, step in ((3, 1), (4, -1)):
                send(own, own, ag_send.at[a, h, n], ag_recv.at[a, h, n], along(outer[h], step))

    def gather_relay(a):
        for h in range(2):
            for n, step, lanes in ((3, 1, low), (4, -1, high)):
                sems = (ag_send.at[a, h, n], ag_recv.at[a, h, n])
                arrive(slab(gathered, a, h, -step, whole), *sems, along(outer[h], step))
                sems = (ag_send.at[a, h, n + 2], ag_recv.at[a, h, n + 2])
                passed = slab(gathered, a, h, -step, lanes)
                send(passed, passed, *sems, along(outer[h], step))

    def gather_end(a):
        for h in range(2):
            for n, step, lanes in ((5, 1, low), (6, -1, high)):
                sems = (ag_send.at[a, h, n], ag_recv.at[a, h, n])
                arrive(slab(gathered, a, h, -2 * step, lanes), *sems, along(outer[h], step))

    def scatter_start(p, h):
        def put(n, step, lanes, target, to):
            send(
                slab(partial, p, h, step, lanes), target.at[p, h, :, :, lanes],
                rs_send.at[p, h, n], rs_recv.at[p, h, n], along(outer[h], to),
            )

        put(0, 2, low, pass_on, 1)
        put(1, 2, high, pass_on, -1)
        put(2, 1, high, from_prev, 1)
        put(3, -1, low, from_next, -1)

    def scatter_relay(p):
        for h in range(2):
            for n, step, lanes, target in ((0, 1, low, from_prev), (1, -1, high, from_next)):
                passing = pass_on.at[p, h, :, :, lanes]
                arrive(passing, rs_send.at[p, h, n], rs_recv.at[p, h, n], along(outer[h], step))
                mine = slab(partial, p, h, step, lanes)
                mine[...] = (mine[...].astype(F32) + passing[...].astype(F32)).astype(BF16)
                send(
                    mine, target.at[p, h, :, :, lanes],
                    rs_send.at[p, h, n + 4], rs_recv.at[p, h, n + 4], along(outer[h], step),
                )

    def scatter_inner(p):
        for h in range(2):
            for n, lanes, target, step in (
                (2, high, from_prev, 1), (3, low, from_next, -1), (4, low, from_prev, 1), (5, high, from_next, -1),
            ):
                landed = target.at[p, h, :, :, lanes]
                arrive(landed, rs_send.at[p, h, n], rs_recv.at[p, h, n], along(outer[h], step))
            total = slab(partial, p, h, 0, whole)[...].astype(F32)
            total = total + from_prev[p, h].astype(F32) + from_next[p, h].astype(F32)
            summed[p, h] = total.astype(BF16)
            for step in (1, 3, 2):
                at = (place[inner[h]] + step) % RING
                send(
                    summed.at[p, h, at], scattered.at[p, h, step - 1],
                    rs_send.at[p, h, 5 + step], rs_recv.at[p, h, 5 + step], along(inner[h], step),
                )

    def scatter_end(p):
        halves = []
        for h in range(2):
            total = summed[p, h, pl.ds(place[inner[h]], 1)][0].astype(F32)
            for step in (1, 2, 3):
                landed = scattered.at[p, h, step - 1]
                sems = (rs_send.at[p, h, 5 + step], rs_recv.at[p, h, 5 + step])
                arrive(landed, *sems, along(inner[h], step))
                total = total + landed[...].astype(F32)
            halves.append(total)
        return jnp.concatenate(halves, axis=1)

    def put_block(a, value):
        value = value.astype(BF16)
        for h in range(2):
            block(gathered, a, h, 0)[...] = value[:, h * width : (h + 1) * width]

    def factor_of(value):
        return lax.rsqrt(mean(value * value) + EPSILON)

    def normed(value):
        return value * factor_of(value) * gain

    def tokens(a, h):
        return gathered[a, h].reshape(RING * RING * 16, width)

    def onto_units(a, weights):
        return contract_last(tokens(a, 0), weights[0]) + contract_last(tokens(a, 1), weights[1])

    def onto_features(p, value, weights):
        tile = 256
        for h in range(2):
            for n in range(width // tile):
                lanes = pl.ds(n * tile, tile)
                product = jnp.dot(value, weights[h, :, lanes], preferred_element_type=F32)
                partial[p, h, :, :, :, lanes] = product.astype(BF16).reshape(RING, RING, 16, tile)
            scatter_start(p, h)

    def forward(p, a):
        hidden = onto_units(a, up)
        active = (hidden * jax.nn.sigmoid(hidden)).astype(BF16)
        onto_features(p, active, down)

    def backward_hidden(period, a):
        hidden = onto_units(a, up)
        gating = jax.nn.sigmoid(hidden)
        active_kept[...] = (hidden * gating).astype(BF16)
        hidden_kept[...] = gating * (1.0 + hidden * (1.0 - gating))
        flipped[1, period] = active_kept[...].T

    def backward(p, period, a):
        slopes[...] = (onto_units(a, down) * hidden_kept[...]).astype(BF16)
        onto_features(p, slopes[...], up)

    def backward_keep(period):
        flipped[0, period] = slopes[...].T

    def weight_grad(kind, h, target, first, second):
        tile = 256
        left = jnp.concatenate([flipped[kind, 0], flipped[kind, 1]], axis=1)
        for n in range(width // tile):
            lanes = pl.ds(n * tile, tile)
            right = jnp.concatenate(
                [gathered[a, h, :, :, :, lanes].reshape(-1, tile) for a in (first, second)], axis=0
            )
            total = jnp.dot(left, right, preferred_element_type=F32)
            target[0, :, pl.ds(h * width + n * tile, tile)] = total.astype(BF16)

    def hop(n, value, to):
        hop_out[n] = value.astype(BF16)
        send(hop_out.at[n], hop_in.at[n], hop_send.at[n], hop_recv.at[n], to)

    def hopped(n, to):
        arrive(hop_in.at[n], hop_send.at[n], hop_recv.at[n], to)
        return hop_in[n].astype(F32)

    def deliver(n, target, period, value):
        value = value.astype(BF16)
        mirror_out[n] = value
        send(mirror_out.at[n], mirror_in.at[n], mirror_send.at[n], mirror_recv.at[n], mirror)
        target[period, 0, 0] = value.astype(F32)[:8].astype(BF16)

    def delivered(n, target, period):
        arrive(mirror_in.at[n], mirror_send.at[n], mirror_recv.at[n], mirror)
        target[period, 1, 0] = mirror_in[n].astype(F32)[8:].astype(BF16)

    def wide(value):
        return value.astype(F32)

    def joined(first, second):
        return jnp.concatenate([wide(first), wide(second)], axis=0)

    far_out[0] = joined(states_in[1, 0], cotangent[1, 0]).astype(BF16)
    send(far_out.at[0], far_in.at[0], far_send.at[0], far_recv.at[0], mirror)
    far_out[1] = joined(saved[0, 1, 0], saved[1, 1, 0]).astype(BF16)
    send(far_out.at[1], far_in.at[1], far_send.at[1], far_recv.at[1], mirror)

    chosen = lax.broadcasted_iota(jnp.int32, gains.shape, 0) == s
    gain = jnp.sum(jnp.where(chosen, wide(gains[...]), 0.0), axis=0, keepdims=True)

    arrive(far_in.at[0], far_send.at[0], far_recv.at[0], mirror)
    far = wide(far_in[0])
    rows[0] = jnp.concatenate([wide(states_in[0, 0]), far[:8]], axis=0)
    put_block(FA, normed(rows[0]))
    gather_inner(FA)
    grads[0] = jnp.concatenate([wide(cotangent[0, 0]), far[8:]], axis=0)
    put_block(GA, grads[0])
    arrive(far_in.at[1], far_send.at[1], far_recv.at[1], mirror)
    far = wide(far_in[1])
    rows[1] = jnp.concatenate([wide(saved[0, 0, 0]), far[:8]], axis=0)
    put_block(NA, normed(rows[1]))
    rows[2] = jnp.concatenate([wide(saved[1, 0, 0]), far[8:]], axis=0)
    put_block(NB, normed(rows[2]))
    gather_outer(FA)
    gather_inner(NA)
    gather_inner(GA)
    gather_relay(FA)
    gather_outer(NA)
    gather_end(FA)
    for load in loads:
        load.wait()
    forward(0, FA)
    gather_relay(NA)
    gather_outer(GA)
    scatter_relay(0)
    gather_end(NA)
    backward_hidden(0, NA)
    gather_relay(GA)
    gather_inner(NB)
    scatter_inner(0)
    gather_end(GA)
    backward(1, 0, GA)
    gather_outer(NB)
    produced = (rows[0] + scatter_end(0)).astype(BF16)
    hop(0, produced, after)
    deliver(0, states_out, 0, produced)
    backward_keep(0)
    gather_relay(NB)
    rows[3] = jnp.where(s == 0, joined(entering[0, 0], entering[0, 1]), hopped(0, after))
    put_block(FB, normed(rows[3]))
    gather_inner(FB)
    scatter_relay(1)
    gather_outer(FB)
    gather_end(NB)
    backward_hidden(1, NB)
    scatter_inner(1)
    gather_relay(FB)

    def returned(n, cot, p):
        scaled = scatter_end(p) * gain
        factor = factor_of(rows[n])
        unit = rows[n] * factor
        return (cot + factor * (scaled - unit * mean(unit * scaled))).astype(BF16)

    back = returned(1, grads[0], 1)
    hop(1, back, before)
    deliver(1, input_grads, 0, back)
    gather_end(FB)
    forward(2, FB)
    grads[1] = jnp.where(
        s == sections - 1, joined(cot_entering[0, 0], cot_entering[0, 1]), hopped(1, before)
    )
    put_block(GB, grads[1])
    gather_inner(GB)
    scatter_relay(2)
    gather_outer(GB)
    gather_relay(GB)
    scatter_inner(2)
    gather_end(GB)
    backward(3, 1, GB)
    produced = (rows[3] + scatter_end(2)).astype(BF16)
    deliver(2, states_out, 1, produced)
    weight_grad(1, 0, grad_down, GA, GB)
    scatter_relay(3)
    weight_grad(1, 1, grad_down, GA, GB)
    backward_keep(1)
    weight_grad(0, 0, grad_up, NA, NB)
    scatter_inner(3)
    weight_grad(0, 1, grad_up, NA, NB)
    back = returned(2, grads[1], 3)
    deliver(3, input_grads, 1, back)
    for n, target, period in (
        (0, states_out, 0), (1, input_grads, 0), (2, states_out, 1), (3, input_grads, 1),
    ):
        delivered(n, target, period)
    for copy in sends:
        copy.wait_send()


def write_out(*refs):
    sems = refs[-1]
    copies = [pltpu.make_async_copy(refs[n], refs[4 + n], sems.at[n]) for n in range(4)]
    for copy in copies:
        copy.start()
    for copy in copies:
        copy.wait()


def body(states_in, entering, saved, cotangent, cot_entering, gains, up_rows, down_rows):
    units, features = up_rows.shape[2:]
    width = features // 2
    dma, vmem = pltpu.SemaphoreType.DMA, pltpu.VMEM
    in_vmem = pl.BlockSpec(memory_space=pltpu.VMEM)
    anywhere = pl.BlockSpec(memory_space=pl.ANY)
    grid_rows = (RING, RING, 16, width)
    shapes = (saved.shape, saved.shape, (1, units, features), (1, units, features))
    results = pl.pallas_call(
        kernel,
        out_shape=tuple(vmem(shape, BF16) for shape in shapes),
        in_specs=[in_vmem] * 6 + [anywhere] * 2,
        out_specs=(in_vmem,) * 4,
        scratch_shapes=[
            vmem((2, units, width), BF16),
            vmem((2, units, width), BF16),
            vmem((6, 2) + grid_rows, BF16),
            vmem((4, 2) + grid_rows, BF16),
            vmem((4, 2) + grid_rows[1:], BF16),
            vmem((4, 2) + grid_rows[1:], BF16),
            vmem((4, 2) + grid_rows[1:], BF16),
            vmem((4, 2) + grid_rows[1:], BF16),
            vmem((4, 2, 3, 16, width), BF16),
            vmem((4, 16, features), F32),
            vmem((2, 16, features), F32),
            vmem((2, 16, features), BF16),
            vmem((2, 16, features), BF16),
            vmem((2, 16, features), BF16),
            vmem((2, 16, features), BF16),
            vmem((4, 16, features), BF16),
            vmem((4, 16, features), BF16),
            vmem((256, units), BF16),
            vmem((256, units), F32),
            vmem((256, units), BF16),
            vmem((2, 2, units, 256), BF16),
            dma((4,)),
            dma((6, 2, 7)),
            dma((6, 2, 7)),
            dma((4, 2, 9)),
            dma((4, 2, 9)),
            dma((2,)),
            dma((2,)),
            dma((2,)),
            dma((2,)),
            dma((4,)),
            dma((4,)),
        ],
        compiler_params=pltpu.CompilerParams(
            collective_id=0, has_side_effects=True, vmem_limit_bytes=48 * 2**20
        ),
        cost_estimate=pl.CostEstimate(flops=15 * 10**9, bytes_accessed=17 * 10**6, transcendentals=0),
    )(states_in, entering, saved, cotangent, cot_entering, gains, up_rows, down_rows)
    return pl.pallas_call(
        write_out,
        out_shape=tuple(jax.ShapeDtypeStruct(shape, BF16) for shape in shapes),
        in_specs=[in_vmem] * 4,
        out_specs=(anywhere,) * 4,
        scratch_shapes=[dma((4,))],
        compiler_params=pltpu.CompilerParams(vmem_limit_bytes=4 * 2**20),
    )(*results)


def solution(mesh):
    group = ("dp", "tensor")
    placed = (
        P(None, "section", group, None),
        P(None, None, group, None),
        P(None, None, "section", group, None),
        P(None, "section", group, None),
        P(None, None, group, None),
        P(),
        P("section", None, group, None),
        P("section", None, group, None),
    )
    return jax.shard_map(
        body,
        mesh=mesh,
        in_specs=placed,
        out_specs=(
            P(None, None, "section", group, None),
            P(None, None, "section", group, None),
            P("section", group, None),
            P("section", group, None),
        ),
        check_vma=False,
    )
```

```python
import functools

import jax
import jax.numpy as jnp
from jax import lax
from jax.experimental import pallas as pl
from jax.experimental.pallas import tpu as pltpu
from jax.sharding import PartitionSpec as P

EPSILON = 1e-06
MESH = pl.DeviceIdType.MESH
F32, BF16 = jnp.float32, jnp.bfloat16
FA, NA, GA, NB, FB, GB = range(6)
FS, NS, GS = (FA, FB), (NA, NB), (GA, GB)
RING = 4

ORDER = (
    "far0", "far1", "far2", "nF0", "nG0", "nN0", "outF0", "outN0", "relF0", "outG0", "relN0",
    "relG0", "hF0", "pF0h0", "pF0h1", "hB0", "nN1", "gB0", "rsrF0", "pB0h0", "pB0h1", "rsiF0",
    "rsrB0", "outN1", "finF0", "rsiB0", "nF1", "relN1", "finB0", "outF1", "nG1", "hB1", "relF1",
    "outG1", "hF1", "relG1", "pF1h0", "pF1h1", "gB1", "rsrF1", "pB1h0", "pB1h1", "w1a", "keepB1",
    "rsrB1", "rsiF1", "w1b", "keepB0", "rsiB1", "w0a", "finF1", "finB1", "w0b", "end",
)


def contract_last(former, latter):
    return lax.dot_general(former, latter, (((1,), (1,)), ((), ())), preferred_element_type=F32)


def mean(value):
    return jnp.mean(value, axis=-1, keepdims=True)


def kernel(
    states_in, entering, saved, cotangent, cot_entering, gains, up_rows, down_rows,
    states_out, input_grads, grad_up, grad_down,
    up, down, gathered, partial, pass_on, from_prev, from_next, summed, scattered,
    rows, far_out, far_in, hop_out, hop_in, mirror_out, mirror_in,
    slopes, bent, active, flipped,
    load_sem, ag_send, ag_recv, rs_send, rs_recv, far_send, far_recv,
    hop_send, hop_recv, mirror_send, mirror_recv,
):
    s = lax.axis_index("section")
    d = lax.axis_index("dp")
    t = lax.axis_index("tensor")
    sections = lax.axis_size("section")
    width = up.shape[-1]
    half = width // 2
    features = 2 * width
    units = up.shape[1]
    place = {"x": d % RING, "z": (d // RING) * 2 + t}

    def device(section, x, z):
        return (section, (z // 2) * RING + x, z % 2)

    def along(axis, step):
        moved = dict(place)
        moved[axis] = (place[axis] + step) % RING
        return device(s, moved["x"], moved["z"])

    mirror = device(sections - 1 - s, place["x"], place["z"])
    after = device((s + 1) % sections, place["x"], place["z"])
    before = device((s + sections - 1) % sections, place["x"], place["z"])

    loads = [
        pltpu.make_async_copy(
            source.at[0, 0, :, pl.ds(h * width, width)], target.at[h], load_sem.at[2 * n + h]
        )
        for n, (source, target) in enumerate(((up_rows, up), (down_rows, down)))
        for h in range(2)
    ]
    for load in loads:
        load.start()

    barrier = pltpu.get_barrier_semaphore()
    partners = [along(axis, step) for axis in "xz" for step in (1, 2, 3)] + [mirror, after, before]
    for partner in partners:
        pl.semaphore_signal(barrier, inc=1, device_id=partner, device_id_type=MESH)
    pl.semaphore_wait(barrier, len(partners))

    sends = []

    def send(source, target, send_sem, recv_sem, device_id):
        copy = pltpu.make_async_remote_copy(
            src_ref=source, dst_ref=target, send_sem=send_sem, recv_sem=recv_sem,
            device_id=device_id, device_id_type=MESH,
        )
        copy.start()
        sends.append(copy)

    def arrive(target, send_sem, recv_sem, device_id):
        pltpu.make_async_remote_copy(
            src_ref=target, dst_ref=target, send_sem=send_sem, recv_sem=recv_sem,
            device_id=device_id, device_id_type=MESH,
        ).wait_recv()

    inner, outer = ("x", "z"), ("z", "x")
    low, high, whole = pl.ds(0, half), pl.ds(half, half), pl.ds(0, width)

    def slab(ref, index, h, step, lanes):
        at = (place[outer[h]] + step) % RING
        return ref.at[index, h, at, :, :, lanes] if h == 0 else ref.at[index, h, :, at, :, lanes]

    def block(ref, index, h, step):
        at = dict(place)
        at[inner[h]] = (place[inner[h]] + step) % RING
        return ref.at[index, h, at["z"], at["x"]]

    def gather_inner(a):
        for h in range(2):
            for step in (1, 3, 2):
                own = block(gathered, a, h, 0)
                sems = (ag_send.at[a, h, step - 1], ag_recv.at[a, h, step - 1])
                send(own, own, *sems, along(inner[h], step))

    def gather_outer(a):
        for h in range(2):
            for step in (1, 2, 3):
                sems = (ag_send.at[a, h, step - 1], ag_recv.at[a, h, step - 1])
                arrive(block(gathered, a, h, -step), *sems, along(inner[h], step))
        for group in (((3, 1, low), (4, -1, high)), ((7, 1, high), (8, -1, low))):
            for h in range(2):
                for n, step, lanes in group:
                    own = slab(gathered, a, h, 0, lanes)
                    send(own, own, ag_send.at[a, h, n], ag_recv.at[a, h, n], along(outer[h], step))

    def gather_relay(a):
        for h in range(2):
            for n, step, lanes in ((3, 1, low), (4, -1, high)):
                passed = slab(gathered, a, h, -step, lanes)
                arrive(passed, ag_send.at[a, h, n], ag_recv.at[a, h, n], along(outer[h], step))
                sems = (ag_send.at[a, h, n + 2], ag_recv.at[a, h, n + 2])
                send(passed, passed, *sems, along(outer[h], step))

    def gather_end(a):
        for h in range(2):
            for n, step, lanes, far in ((5, 1, low, 2), (6, -1, high, 2), (7, 1, high, 1), (8, -1, low, 1)):
                sems = (ag_send.at[a, h, n], ag_recv.at[a, h, n])
                arrive(slab(gathered, a, h, -far * step, lanes), *sems, along(outer[h], step))

    def scatter_start(p, h):
        def put(n, step, lanes, target, to):
            send(
                slab(partial, p, h, step, lanes), target.at[p, h, :, :, lanes],
                rs_send.at[p, h, n], rs_recv.at[p, h, n], along(outer[h], to),
            )

        put(0, 2, low, pass_on, 1)
        put(1, 2, high, pass_on, -1)
        put(2, 1, high, from_prev, 1)
        put(3, -1, low, from_next, -1)

    def scatter_relay(p):
        for h in range(2):
            for n, step, lanes, target in ((0, 1, low, from_prev), (1, -1, high, from_next)):
                passing = pass_on.at[p, h, :, :, lanes]
                arrive(passing, rs_send.at[p, h, n], rs_recv.at[p, h, n], along(outer[h], step))
                mine = slab(partial, p, h, step, lanes)
                mine[...] = (mine[...].astype(F32) + passing[...].astype(F32)).astype(BF16)
                send(
                    mine, target.at[p, h, :, :, lanes],
                    rs_send.at[p, h, n + 4], rs_recv.at[p, h, n + 4], along(outer[h], step),
                )

    def scatter_inner(p):
        for h in range(2):
            for n, lanes, target, step in (
                (2, high, from_prev, 1), (3, low, from_next, -1), (4, low, from_prev, 1), (5, high, from_next, -1),
            ):
                landed = target.at[p, h, :, :, lanes]
                arrive(landed, rs_send.at[p, h, n], rs_recv.at[p, h, n], along(outer[h], step))
            total = slab(partial, p, h, 0, whole)[...].astype(F32)
            total = total + from_prev[p, h].astype(F32) + from_next[p, h].astype(F32)
            summed[p, h] = total.astype(BF16)
            for step in (1, 3, 2):
                at = (place[inner[h]] + step) % RING
                send(
                    summed.at[p, h, at], scattered.at[p, h, step - 1],
                    rs_send.at[p, h, 5 + step], rs_recv.at[p, h, 5 + step], along(inner[h], step),
                )

    def scatter_end(p):
        halves = []
        for h in range(2):
            total = summed[p, h, pl.ds(place[inner[h]], 1)][0].astype(F32)
            for step in (1, 2, 3):
                landed = scattered.at[p, h, step - 1]
                sems = (rs_send.at[p, h, 5 + step], rs_recv.at[p, h, 5 + step])
                arrive(landed, *sems, along(inner[h], step))
                total = total + landed[...].astype(F32)
            halves.append(total)
        return jnp.concatenate(halves, axis=1)

    def put_block(a, value):
        value = value.astype(BF16)
        for h in range(2):
            block(gathered, a, h, 0)[...] = value[:, h * width : (h + 1) * width]

    def factor_of(value):
        return lax.rsqrt(mean(value * value) + EPSILON)

    def normed(value):
        return value * factor_of(value) * gain

    def tokens(a, h):
        return gathered[a, h].reshape(RING * RING * 16, width)

    def onto_units(a, weights):
        return contract_last(tokens(a, 0), weights[0]) + contract_last(tokens(a, 1), weights[1])

    def onto_features(p, h, value, weights):
        tile = 256
        for n in range(width // tile):
            lanes = pl.ds(n * tile, tile)
            product = jnp.dot(value, weights[h, :, lanes], preferred_element_type=F32)
            partial[p, h, :, :, :, lanes] = product.astype(BF16).reshape(RING, RING, 16, tile)
        scatter_start(p, h)

    loaded = set()

    def weights_of(n):
        if n not in loaded:
            loaded.add(n)
            for load in loads[2 * n : 2 * n + 2]:
                load.wait()
        return (up, down)[n]

    def hidden_forward(period):
        gather_end(FS[period])
        hidden = onto_units(FS[period], weights_of(0))
        active[...] = (hidden * jax.nn.sigmoid(hidden)).astype(BF16)

    def hidden_backward(period):
        gather_end(NS[period])
        hidden = onto_units(NS[period], weights_of(0))
        gating = jax.nn.sigmoid(hidden)
        flipped[1, period] = (hidden * gating).astype(BF16).T
        bent[period] = gating * (1.0 + hidden * (1.0 - gating))

    def slope(period):
        gather_end(GS[period])
        slopes[period] = (onto_units(GS[period], weights_of(1)) * bent[period]).astype(BF16)

    def keep_slope(period):
        flipped[0, period] = slopes[period].T

    def weight_grad(kind, h, target, first, second):
        tile = 256
        left = jnp.concatenate([flipped[kind, 0], flipped[kind, 1]], axis=1)
        for n in range(width // tile):
            lanes = pl.ds(n * tile, tile)
            right = jnp.concatenate(
                [gathered[a, h, :, :, :, lanes].reshape(-1, tile) for a in (first, second)], axis=0
            )
            total = jnp.dot(left, right, preferred_element_type=F32)
            target[0, :, pl.ds(h * width + n * tile, tile)] = total.astype(BF16)

    def wide(value):
        return value.astype(F32)

    def folded(value):
        return jnp.concatenate([wide(value)[:, :width], wide(value)[:, width:]], axis=0).astype(BF16)

    def unfolded(value):
        return jnp.concatenate([wide(value)[:8], wide(value)[8:]], axis=1)

    def far_send_one(n, value):
        far_out[n] = folded(value)
        send(far_out.at[n], far_in.at[n], far_send.at[n], far_recv.at[n], mirror)

    def with_far(own, n):
        arrive(far_in.at[n], far_send.at[n], far_recv.at[n], mirror)
        return jnp.concatenate([wide(own), unfolded(far_in[n])], axis=0)

    def hop(n, value, to):
        hop_out[n] = value
        send(hop_out.at[n], hop_in.at[n], hop_send.at[n], hop_recv.at[n], to)

    def hopped(n, to):
        arrive(hop_in.at[n], hop_send.at[n], hop_recv.at[n], to)
        return wide(hop_in[n])

    def deliver(n, target, period, value):
        mirror_out[n] = folded(value[8:])
        send(mirror_out.at[n], mirror_in.at[n], mirror_send.at[n], mirror_recv.at[n], mirror)
        target[period, 0, 0] = value[:8].astype(BF16)

    def delivered(n, target, period):
        arrive(mirror_in.at[n], mirror_send.at[n], mirror_recv.at[n], mirror)
        target[period, 1, 0] = unfolded(mirror_in[n]).astype(BF16)

    def rounded(value):
        return wide(value.astype(BF16))

    def finish_forward(period):
        p = 2 * period
        produced = rounded(rows[FS[period]] + scatter_end(p))
        if period == 0:
            hop(0, produced.astype(BF16), after)
        deliver(p, states_out, period, produced)

    def finish_backward(period):
        p = 2 * period + 1
        scaled = scatter_end(p) * gain
        own = rows[NS[period]]
        factor = factor_of(own)
        unit = own * factor
        back = factor * (scaled - unit * mean(unit * scaled))
        back = rounded(rows[GS[period]] + back)
        if period == 0:
            hop(1, back.astype(BF16), before)
        deliver(p, input_grads, period, back)

    def begin(a, value):
        rows[a] = value
        put_block(a, value if a in GS else normed(value))
        gather_inner(a)

    def joined(pair):
        return jnp.concatenate([wide(pair[0]), wide(pair[1])], axis=0)

    def begin_later_forward():
        begin(FB, jnp.where(s == 0, joined(entering[0]), hopped(0, after)))

    def begin_later_grads():
        begin(GB, jnp.where(s == sections - 1, joined(cot_entering[0]), hopped(1, before)))

    def far_saved():
        far_send_one(2, saved[0, 1, 0])
        far_send_one(3, saved[1, 1, 0])

    def end():
        for n, target in enumerate((states_out, input_grads) * 2):
            delivered(n, target, n // 2)
        for copy in sends:
            copy.wait_send()

    chosen = lax.broadcasted_iota(jnp.int32, gains.shape, 0) == s
    gain = jnp.sum(jnp.where(chosen, wide(gains[...]), 0.0), axis=0, keepdims=True)
    steps = {
        "far0": lambda: far_send_one(0, states_in[1, 0]),
        "far1": lambda: far_send_one(1, cotangent[1, 0]),
        "far2": far_saved,
        "nF0": lambda: begin(FA, with_far(states_in[0, 0], 0)),
        "nG0": lambda: begin(GA, with_far(cotangent[0, 0], 1)),
        "nN0": lambda: begin(NA, with_far(saved[0, 0, 0], 2)),
        "nN1": lambda: begin(NB, with_far(saved[1, 0, 0], 3)),
        "nF1": begin_later_forward,
        "nG1": begin_later_grads,
        "w1a": lambda: weight_grad(1, 0, grad_down, GA, GB),
        "w1b": lambda: weight_grad(1, 1, grad_down, GA, GB),
        "w0a": lambda: weight_grad(0, 0, grad_up, NA, NB),
        "w0b": lambda: weight_grad(0, 1, grad_up, NA, NB),
        "end": end,
    }
    for a, name in enumerate(("F0", "N0", "G0", "N1", "F1", "G1")):
        steps["out" + name] = functools.partial(gather_outer, a)
        steps["rel" + name] = functools.partial(gather_relay, a)
    for period in range(2):
        k = str(period)
        steps["hF" + k] = functools.partial(hidden_forward, period)
        steps["hB" + k] = functools.partial(hidden_backward, period)
        steps["gB" + k] = functools.partial(slope, period)
        steps["keepB" + k] = functools.partial(keep_slope, period)
        steps["finF" + k] = functools.partial(finish_forward, period)
        steps["finB" + k] = functools.partial(finish_backward, period)
        for h in range(2):
            steps[f"pF{k}h{h}"] = lambda p=2 * period, h=h: onto_features(p, h, active[...], weights_of(1))
            steps[f"pB{k}h{h}"] = lambda p=2 * period + 1, h=h: onto_features(
                p, h, slopes[p // 2], weights_of(0)
            )
        for n, name in enumerate("FB"):
            steps["rsr" + name + k] = functools.partial(scatter_relay, 2 * period + n)
            steps["rsi" + name + k] = functools.partial(scatter_inner, 2 * period + n)
    for name in ORDER:
        steps[name]()


def write_out(*refs):
    sems = refs[-1]
    copies = [pltpu.make_async_copy(refs[n], refs[4 + n], sems.at[n]) for n in range(4)]
    for copy in copies:
        copy.start()
    for copy in copies:
        copy.wait()


def body(states_in, entering, saved, cotangent, cot_entering, gains, up_rows, down_rows):
    units, features = up_rows.shape[2:]
    width = features // 2
    dma, vmem = pltpu.SemaphoreType.DMA, pltpu.VMEM
    in_vmem = pl.BlockSpec(memory_space=pltpu.VMEM)
    anywhere = pl.BlockSpec(memory_space=pl.ANY)
    grid_rows = (RING, RING, 16, width)
    shapes = (saved.shape, saved.shape, (1, units, features), (1, units, features))
    results = pl.pallas_call(
        kernel,
        out_shape=tuple(vmem(shape, BF16) for shape in shapes),
        in_specs=[in_vmem] * 6 + [anywhere] * 2,
        out_specs=(in_vmem,) * 4,
        scratch_shapes=[
            vmem((2, units, width), BF16),
            vmem((2, units, width), BF16),
            vmem((6, 2) + grid_rows, BF16),
            vmem((4, 2) + grid_rows, BF16),
            vmem((4, 2) + grid_rows[1:], BF16),
            vmem((4, 2) + grid_rows[1:], BF16),
            vmem((4, 2) + grid_rows[1:], BF16),
            vmem((4, 2) + grid_rows[1:], BF16),
            vmem((4, 2, 3, 16, width), BF16),
            vmem((6, 16, features), F32),
            vmem((4, 16, width), BF16),
            vmem((4, 16, width), BF16),
            vmem((2, 16, features), BF16),
            vmem((2, 16, features), BF16),
            vmem((4, 16, width), BF16),
            vmem((4, 16, width), BF16),
            vmem((2, 256, units), BF16),
            vmem((2, 256, units), F32),
            vmem((256, units), BF16),
            vmem((2, 2, units, 256), BF16),
            dma((4,)),
            dma((6, 2, 9)),
            dma((6, 2, 9)),
            dma((4, 2, 9)),
            dma((4, 2, 9)),
            dma((4,)),
            dma((4,)),
            dma((2,)),
            dma((2,)),
            dma((4,)),
            dma((4,)),
        ],
        compiler_params=pltpu.CompilerParams(
            collective_id=0, has_side_effects=True, vmem_limit_bytes=48 * 2**20
        ),
        cost_estimate=pl.CostEstimate(flops=15 * 10**9, bytes_accessed=17 * 10**6, transcendentals=0),
    )(states_in, entering, saved, cotangent, cot_entering, gains, up_rows, down_rows)
    return pl.pallas_call(
        write_out,
        out_shape=tuple(jax.ShapeDtypeStruct(shape, BF16) for shape in shapes),
        in_specs=[in_vmem] * 4,
        out_specs=(anywhere,) * 4,
        scratch_shapes=[dma((4,))],
        compiler_params=pltpu.CompilerParams(vmem_limit_bytes=4 * 2**20),
    )(*results)


def solution(mesh):
    group = ("dp", "tensor")
    placed = (
        P(None, "section", group, None),
        P(None, None, group, None),
        P(None, None, "section", group, None),
        P(None, "section", group, None),
        P(None, None, group, None),
        P(),
        P("section", None, group, None),
        P("section", None, group, None),
    )
    return jax.shard_map(
        body,
        mesh=mesh,
        in_specs=placed,
        out_specs=(
            P(None, None, "section", group, None),
            P(None, None, "section", group, None),
            P("section", group, None),
            P("section", group, None),
        ),
        check_vma=False,
    )
```

```python
import functools

import jax
import jax.numpy as jnp
from jax import lax
from jax.experimental import pallas as pl
from jax.experimental.pallas import tpu as pltpu
from jax.sharding import PartitionSpec as P

EPSILON = 1e-06
MESH = pl.DeviceIdType.MESH
F32, BF16 = jnp.float32, jnp.bfloat16
FA, NA, GA, NB, FB, GB = range(6)
FS, NS, GS = (FA, FB), (NA, NB), (GA, GB)
RING = 4

ORDER = (
    "far0", "far1", "far2", "nF0", "nG0", "nN0", "outF0", "outN0", "relF0", "outG0", "relN0",
    "relG0", "hF0", "pF0h0", "pF0h1", "hB0", "nN1", "gB0", "rsrF0", "pB0h0", "pB0h1", "rsiF0",
    "rsrB0", "outN1", "finF0", "rsiB0", "nF1", "relN1", "finB0", "outF1", "nG1", "hB1", "relF1",
    "outG1", "hF1", "relG1", "pF1h0", "pF1h1", "gB1", "rsrF1", "pB1h0", "pB1h1", "w1a", "keepB1",
    "rsrB1", "rsiF1", "w1b", "keepB0", "rsiB1", "w0a", "finF1", "finB1", "w0b", "end",
)


def contract_last(former, latter):
    return lax.dot_general(former, latter, (((1,), (1,)), ((), ())), preferred_element_type=F32)


def mean(value):
    return jnp.mean(value, axis=-1, keepdims=True)


def kernel(
    states_in, entering, saved, cotangent, cot_entering, gains, up_rows, down_rows,
    states_out, input_grads, grad_up, grad_down,
    up, down, gathered, partial, pass_on, from_prev, from_next, summed, scattered,
    rows, far_out, far_in, hop_out, hop_in, mirror_out, mirror_in,
    slopes, bent, active, flipped,
    load_sem, ag_send, ag_recv, rs_send, rs_recv, far_send, far_recv,
    hop_send, hop_recv, mirror_send, mirror_recv,
):
    s = lax.axis_index("section")
    d = lax.axis_index("dp")
    t = lax.axis_index("tensor")
    sections = lax.axis_size("section")
    width = up.shape[-1]
    half = width // 2
    features = 2 * width
    units = up.shape[1]
    place = {"x": d % RING, "z": (d // RING) * 2 + t}

    def device(section, x, z):
        return (section, (z // 2) * RING + x, z % 2)

    def moved(axis, step):
        to = dict(place)
        to[axis] = (place[axis] + step) % RING
        return device(s, to["x"], to["z"])

    neighbours = {(axis, step): moved(axis, step) for axis in "xz" for step in (1, 2, 3)}

    def along(axis, step):
        return neighbours[axis, step % RING]

    mirror = device(sections - 1 - s, place["x"], place["z"])
    after = device((s + 1) % sections, place["x"], place["z"])
    before = device((s + sections - 1) % sections, place["x"], place["z"])

    loads = [
        pltpu.make_async_copy(
            source.at[0, 0, :, pl.ds(h * width, width)], target.at[h], load_sem.at[2 * n + h]
        )
        for n, (source, target) in enumerate(((up_rows, up), (down_rows, down)))
        for h in range(2)
    ]
    for load in loads:
        load.start()

    barrier = pltpu.get_barrier_semaphore()
    partners = [along(axis, step) for axis in "xz" for step in (1, 2, 3)] + [mirror, after, before]
    for partner in partners:
        pl.semaphore_signal(barrier, inc=1, device_id=partner, device_id_type=MESH)
    pl.semaphore_wait(barrier, len(partners))

    def send(source, target, send_sem, recv_sem, device_id):
        pltpu.make_async_remote_copy(
            src_ref=source, dst_ref=target, send_sem=send_sem, recv_sem=recv_sem,
            device_id=device_id, device_id_type=MESH,
        ).start()

    def arrived(like, recv_sem):
        pltpu.make_async_remote_copy(
            src_ref=like, dst_ref=like, send_sem=recv_sem, recv_sem=recv_sem,
            device_id=mirror, device_id_type=MESH,
        ).wait_recv()

    def departed(like, send_sem):
        pltpu.make_async_remote_copy(
            src_ref=like, dst_ref=like, send_sem=send_sem, recv_sem=send_sem,
            device_id=mirror, device_id_type=MESH,
        ).wait_send()

    blocks = {6: scattered.at[0], 8: from_prev.at[0], 16: from_prev.at[0:2], 24: from_prev.at[0:3]}

    inner, outer = ("x", "z"), ("z", "x")
    low, high, whole = pl.ds(0, half), pl.ds(half, half), pl.ds(0, width)

    def slab(ref, index, h, step, lanes):
        at = (place[outer[h]] + step) % RING
        return ref.at[index, h, at, :, :, lanes] if h == 0 else ref.at[index, h, :, at, :, lanes]

    def block(ref, index, h, step):
        at = dict(place)
        at[inner[h]] = (place[inner[h]] + step) % RING
        return ref.at[index, h, at["z"], at["x"]]

    def gather_inner(a):
        for step in (1, 3, 2):
            for h in range(2):
                own = block(gathered, a, h, 0)
                send(own, own, ag_send.at[a, 0], ag_recv.at[a, 0], along(inner[h], step))

    def gather_outer(a):
        arrived(blocks[6], ag_recv.at[a, 0])
        for n, group in ((1, ((1, low), (-1, high))), (2, ((1, high), (-1, low)))):
            for h in range(2):
                for step, lanes in group:
                    own = slab(gathered, a, h, 0, lanes)
                    send(own, own, ag_send.at[a, 1], ag_recv.at[a, n], along(outer[h], step))

    def gather_relay(a):
        arrived(blocks[8], ag_recv.at[a, 1])
        for h in range(2):
            for step, lanes in ((1, low), (-1, high)):
                passed = slab(gathered, a, h, -step, lanes)
                send(passed, passed, ag_send.at[a, 1], ag_recv.at[a, 2], along(outer[h], step))

    def gather_end(a):
        arrived(blocks[16], ag_recv.at[a, 2])

    def scatter_start(p, h):
        for n, step, lanes, target, to in (
            (0, 2, low, pass_on, 1),
            (0, 2, high, pass_on, -1),
            (1, 1, high, from_prev, 1),
            (1, -1, low, from_next, -1),
        ):
            send(
                slab(partial, p, h, step, lanes), target.at[p, h, :, :, lanes],
                rs_send.at[p, 1], rs_recv.at[p, n], along(outer[h], to),
            )

    def scatter_relay(p):
        arrived(blocks[8], rs_recv.at[p, 0])
        for h in range(2):
            for step, lanes, target in ((1, low, from_prev), (-1, high, from_next)):
                mine = slab(partial, p, h, step, lanes)
                passing = pass_on[p, h, :, :, lanes].astype(F32)
                mine[...] = (mine[...].astype(F32) + passing).astype(BF16)
                send(
                    mine, target.at[p, h, :, :, lanes],
                    rs_send.at[p, 1], rs_recv.at[p, 1], along(outer[h], step),
                )

    def scatter_inner(p):
        arrived(blocks[16], rs_recv.at[p, 1])
        for h in range(2):
            total = slab(partial, p, h, 0, whole)[...].astype(F32)
            total = total + from_prev[p, h].astype(F32) + from_next[p, h].astype(F32)
            summed[p, h] = total.astype(BF16)
            for step in (1, 3, 2):
                at = (place[inner[h]] + step) % RING
                send(
                    summed.at[p, h, at], scattered.at[p, h, step - 1],
                    rs_send.at[p, 0], rs_recv.at[p, 2], along(inner[h], step),
                )

    def scatter_end(p):
        arrived(blocks[6], rs_recv.at[p, 2])
        halves = []
        for h in range(2):
            total = summed[p, h, pl.ds(place[inner[h]], 1)][0].astype(F32)
            for step in (1, 2, 3):
                total = total + scattered[p, h, step - 1].astype(F32)
            halves.append(total)
        return jnp.concatenate(halves, axis=1)

    def put_block(a, value):
        value = value.astype(BF16)
        for h in range(2):
            block(gathered, a, h, 0)[...] = value[:, h * width : (h + 1) * width]

    def factor_of(value):
        return lax.rsqrt(mean(value * value) + EPSILON)

    def normed(value):
        return value * factor_of(value) * gain

    def tokens(a, h):
        return gathered[a, h].reshape(RING * RING * 16, width)

    def onto_units(a, weights):
        return contract_last(tokens(a, 0), weights[0]) + contract_last(tokens(a, 1), weights[1])

    def onto_features(p, h, value, weights):
        tile = 256
        for n in range(width // tile):
            lanes = pl.ds(n * tile, tile)
            product = jnp.dot(value, weights[h, :, lanes], preferred_element_type=F32)
            partial[p, h, :, :, :, lanes] = product.astype(BF16).reshape(RING, RING, 16, tile)
        scatter_start(p, h)

    loaded = set()

    def weights_of(n):
        if n not in loaded:
            loaded.add(n)
            for load in loads[2 * n : 2 * n + 2]:
                load.wait()
        return (up, down)[n]

    def hidden_forward(period):
        gather_end(FS[period])
        hidden = onto_units(FS[period], weights_of(0))
        active[...] = (hidden * jax.nn.sigmoid(hidden)).astype(BF16)

    def hidden_backward(period):
        gather_end(NS[period])
        hidden = onto_units(NS[period], weights_of(0))
        gating = jax.nn.sigmoid(hidden)
        flipped[1, period] = (hidden * gating).astype(BF16).T
        bent[period] = gating * (1.0 + hidden * (1.0 - gating))

    def slope(period):
        gather_end(GS[period])
        slopes[period] = (onto_units(GS[period], weights_of(1)) * bent[period]).astype(BF16)

    def keep_slope(period):
        flipped[0, period] = slopes[period].T

    def weight_grad(kind, h, target, first, second):
        tile = 256
        left = jnp.concatenate([flipped[kind, 0], flipped[kind, 1]], axis=1)
        for n in range(width // tile):
            lanes = pl.ds(n * tile, tile)
            right = jnp.concatenate(
                [gathered[a, h, :, :, :, lanes].reshape(-1, tile) for a in (first, second)], axis=0
            )
            total = jnp.dot(left, right, preferred_element_type=F32)
            target[0, :, pl.ds(h * width + n * tile, tile)] = total.astype(BF16)

    def wide(value):
        return value.astype(F32)

    def folded(value):
        return jnp.concatenate([wide(value)[:, :width], wide(value)[:, width:]], axis=0).astype(BF16)

    def unfolded(value):
        return jnp.concatenate([wide(value)[:8], wide(value)[8:]], axis=1)

    def far_send_one(n, value):
        far_out[n] = folded(value)
        send(far_out.at[n], far_in.at[n], far_send.at[0], far_recv.at[n], mirror)

    def with_far(own, n):
        arrived(far_in.at[n], far_recv.at[n])
        return jnp.concatenate([wide(own), unfolded(far_in[n])], axis=0)

    def hop(n, value, to):
        hop_out[n] = value
        send(hop_out.at[n], hop_in.at[n], hop_send.at[0], hop_recv.at[n], to)

    def hopped(n):
        arrived(hop_in.at[n], hop_recv.at[n])
        return wide(hop_in[n])

    def deliver(n, target, period, value):
        mirror_out[n] = folded(value[8:])
        send(mirror_out.at[n], mirror_in.at[n], mirror_send.at[0], mirror_recv.at[n], mirror)
        target[period, 0, 0] = value[:8].astype(BF16)

    def delivered(n, target, period):
        arrived(mirror_in.at[n], mirror_recv.at[n])
        target[period, 1, 0] = unfolded(mirror_in[n]).astype(BF16)

    def rounded(value):
        return wide(value.astype(BF16))

    def finish_forward(period):
        p = 2 * period
        produced = rounded(rows[FS[period]] + scatter_end(p))
        if period == 0:
            hop(0, produced.astype(BF16), after)
        deliver(p, states_out, period, produced)

    def finish_backward(period):
        p = 2 * period + 1
        scaled = scatter_end(p) * gain
        own = rows[NS[period]]
        factor = factor_of(own)
        unit = own * factor
        back = factor * (scaled - unit * mean(unit * scaled))
        back = rounded(rows[GS[period]] + back)
        if period == 0:
            hop(1, back.astype(BF16), before)
        deliver(p, input_grads, period, back)

    def begin(a, value):
        rows[a] = value
        put_block(a, value if a in GS else normed(value))
        gather_inner(a)

    def joined(pair):
        return jnp.concatenate([wide(pair[0]), wide(pair[1])], axis=0)

    def begin_later_forward():
        begin(FB, jnp.where(s == 0, joined(entering[0]), hopped(0)))

    def begin_later_grads():
        begin(GB, jnp.where(s == sections - 1, joined(cot_entering[0]), hopped(1)))

    def far_saved():
        far_send_one(2, saved[0, 1, 0])
        far_send_one(3, saved[1, 1, 0])

    def end():
        for n, target in enumerate((states_out, input_grads) * 2):
            delivered(n, target, n // 2)
        for like, sem in ((far_out, far_send), (hop_out, hop_send), (mirror_out, mirror_send)):
            departed(like, sem.at[0])
        for sem, count in ((ag_send, 6), (rs_send, 4)):
            for n in range(count):
                departed(blocks[6], sem.at[n, 0])
                departed(blocks[24], sem.at[n, 1])

    chosen = lax.broadcasted_iota(jnp.int32, gains.shape, 0) == s
    gain = jnp.sum(jnp.where(chosen, wide(gains[...]), 0.0), axis=0, keepdims=True)
    steps = {
        "far0": lambda: far_send_one(0, states_in[1, 0]),
        "far1": lambda: far_send_one(1, cotangent[1, 0]),
        "far2": far_saved,
        "nF0": lambda: begin(FA, with_far(states_in[0, 0], 0)),
        "nG0": lambda: begin(GA, with_far(cotangent[0, 0], 1)),
        "nN0": lambda: begin(NA, with_far(saved[0, 0, 0], 2)),
        "nN1": lambda: begin(NB, with_far(saved[1, 0, 0], 3)),
        "nF1": begin_later_forward,
        "nG1": begin_later_grads,
        "w1a": lambda: weight_grad(1, 0, grad_down, GA, GB),
        "w1b": lambda: weight_grad(1, 1, grad_down, GA, GB),
        "w0a": lambda: weight_grad(0, 0, grad_up, NA, NB),
        "w0b": lambda: weight_grad(0, 1, grad_up, NA, NB),
        "end": end,
    }
    for a, name in enumerate(("F0", "N0", "G0", "N1", "F1", "G1")):
        steps["out" + name] = functools.partial(gather_outer, a)
        steps["rel" + name] = functools.partial(gather_relay, a)
    for period in range(2):
        k = str(period)
        steps["hF" + k] = functools.partial(hidden_forward, period)
        steps["hB" + k] = functools.partial(hidden_backward, period)
        steps["gB" + k] = functools.partial(slope, period)
        steps["keepB" + k] = functools.partial(keep_slope, period)
        steps["finF" + k] = functools.partial(finish_forward, period)
        steps["finB" + k] = functools.partial(finish_backward, period)
        for h in range(2):
            steps[f"pF{k}h{h}"] = lambda p=2 * period, h=h: onto_features(p, h, active[...], weights_of(1))
            steps[f"pB{k}h{h}"] = lambda p=2 * period + 1, h=h: onto_features(
                p, h, slopes[p // 2], weights_of(0)
            )
        for n, name in enumerate("FB"):
            steps["rsr" + name + k] = functools.partial(scatter_relay, 2 * period + n)
            steps["rsi" + name + k] = functools.partial(scatter_inner, 2 * period + n)
    for name in ORDER:
        steps[name]()


def write_out(*refs):
    sems = refs[-1]
    copies = [pltpu.make_async_copy(refs[n], refs[4 + n], sems.at[n]) for n in range(4)]
    for copy in copies:
        copy.start()
    for copy in copies:
        copy.wait()


def body(states_in, entering, saved, cotangent, cot_entering, gains, up_rows, down_rows):
    units, features = up_rows.shape[2:]
    width = features // 2
    dma, vmem = pltpu.SemaphoreType.DMA, pltpu.VMEM
    in_vmem = pl.BlockSpec(memory_space=pltpu.VMEM)
    anywhere = pl.BlockSpec(memory_space=pl.ANY)
    grid_rows = (RING, RING, 16, width)
    shapes = (saved.shape, saved.shape, (1, units, features), (1, units, features))
    results = pl.pallas_call(
        kernel,
        out_shape=tuple(vmem(shape, BF16) for shape in shapes),
        in_specs=[in_vmem] * 6 + [anywhere] * 2,
        out_specs=(in_vmem,) * 4,
        scratch_shapes=[
            vmem((2, units, width), BF16),
            vmem((2, units, width), BF16),
            vmem((6, 2) + grid_rows, BF16),
            vmem((4, 2) + grid_rows, BF16),
            vmem((4, 2) + grid_rows[1:], BF16),
            vmem((4, 2) + grid_rows[1:], BF16),
            vmem((4, 2) + grid_rows[1:], BF16),
            vmem((4, 2) + grid_rows[1:], BF16),
            vmem((4, 2, 3, 16, width), BF16),
            vmem((6, 16, features), F32),
            vmem((4, 16, width), BF16),
            vmem((4, 16, width), BF16),
            vmem((2, 16, features), BF16),
            vmem((2, 16, features), BF16),
            vmem((4, 16, width), BF16),
            vmem((4, 16, width), BF16),
            vmem((2, 256, units), BF16),
            vmem((2, 256, units), F32),
            vmem((256, units), BF16),
            vmem((2, 2, units, 256), BF16),
            dma((4,)),
            dma((6, 2)),
            dma((6, 3)),
            dma((4, 2)),
            dma((4, 3)),
            dma((1,)),
            dma((4,)),
            dma((1,)),
            dma((2,)),
            dma((1,)),
            dma((4,)),
        ],
        compiler_params=pltpu.CompilerParams(
            collective_id=0, has_side_effects=True, vmem_limit_bytes=48 * 2**20
        ),
        cost_estimate=pl.CostEstimate(flops=15 * 10**9, bytes_accessed=17 * 10**6, transcendentals=0),
    )(states_in, entering, saved, cotangent, cot_entering, gains, up_rows, down_rows)
    return pl.pallas_call(
        write_out,
        out_shape=tuple(jax.ShapeDtypeStruct(shape, BF16) for shape in shapes),
        in_specs=[in_vmem] * 4,
        out_specs=(anywhere,) * 4,
        scratch_shapes=[dma((4,))],
        compiler_params=pltpu.CompilerParams(vmem_limit_bytes=4 * 2**20),
    )(*results)


def solution(mesh):
    group = ("dp", "tensor")
    placed = (
        P(None, "section", group, None),
        P(None, None, group, None),
        P(None, None, "section", group, None),
        P(None, "section", group, None),
        P(None, None, group, None),
        P(),
        P("section", None, group, None),
        P("section", None, group, None),
    )
    return jax.shard_map(
        body,
        mesh=mesh,
        in_specs=placed,
        out_specs=(
            P(None, None, "section", group, None),
            P(None, None, "section", group, None),
            P("section", group, None),
            P("section", group, None),
        ),
        check_vma=False,
    )
```

```python
import functools

import jax
import jax.numpy as jnp
from jax import lax
from jax.experimental import pallas as pl
from jax.experimental.pallas import tpu as pltpu
from jax.sharding import PartitionSpec as P

EPSILON = 1e-06
MESH = pl.DeviceIdType.MESH
F32, BF16 = jnp.float32, jnp.bfloat16
D0, D1, GA, NB, FB, GB = range(6)
NEAR_FORWARD, NEAR_SAVED = 0, 1
FS, NS, GS = (NEAR_FORWARD, FB), (NEAR_SAVED, NB), (GA, GB)
PASSED = (GA, NB, D1,)
RING = 4

ORDER = (
    "far0", "far1", "far2", "nD0", "nD1", "nG0", "outD0", "irD1", "irG0", "relD0", "outD1", "hD0",
    "relD1", "outG0", "nN1", "hD1", "hF0", "relG0", "pF0h0", "pF0h1", "irN1", "hB0", "gB0",
    "rsrF0", "pB0h0", "pB0h1", "rsiF0", "rsrB0", "outN1", "finF0", "rsiB0", "nF1", "relN1",
    "finB0", "outF1", "nG1", "hB1", "relF1", "outG1", "hF1", "relG1", "pF1h0", "pF1h1", "keepB0",
    "gB1", "rsrF1", "pB1h0", "pB1h1", "keepB1", "w1a", "rsrB1", "rsiF1", "w1b", "rsiB1", "w0a",
    "finF1", "finB1", "w0b", "end",
)


def contract_last(former, latter):
    return lax.dot_general(former, latter, (((1,), (1,)), ((), ())), preferred_element_type=F32)


def mean(value):
    return jnp.mean(value, axis=-1, keepdims=True)


def kernel(
    states_in, entering, saved, cotangent, cot_entering, gains, up_rows, down_rows,
    states_out, input_grads, grad_up, grad_down,
    up, down, gathered, partial, pass_on, from_prev, from_next, summed, scattered,
    rows, far_out, far_in, hop_out, hop_in, mirror_out, mirror_in,
    slopes, bent, active, flipped, near,
    load_sem, ag_send, ag_recv, rs_send, rs_recv, far_send, far_recv,
    hop_send, hop_recv, mirror_send, mirror_recv,
):
    s = lax.axis_index("section")
    d = lax.axis_index("dp")
    t = lax.axis_index("tensor")
    sections = lax.axis_size("section")
    width = up.shape[-1]
    half = width // 2
    features = 2 * width
    units = up.shape[1]
    place = {"x": d % RING, "z": (d // RING) * 2 + t}

    def device(section, x, z):
        return (section, (z // 2) * RING + x, z % 2)

    def moved(axis, step):
        to = dict(place)
        to[axis] = (place[axis] + step) % RING
        return device(s, to["x"], to["z"])

    neighbours = {(axis, step): moved(axis, step) for axis in "xz" for step in (1, 2, 3)}

    def along(axis, step):
        return neighbours[axis, step % RING]

    mirror = device(sections - 1 - s, place["x"], place["z"])
    after = device((s + 1) % sections, place["x"], place["z"])
    before = device((s + sections - 1) % sections, place["x"], place["z"])

    loads = [
        pltpu.make_async_copy(
            source.at[0, 0, :, pl.ds(h * width, width)], target.at[h], load_sem.at[2 * n + h]
        )
        for n, (source, target) in enumerate(((up_rows, up), (down_rows, down)))
        for h in range(2)
    ]
    for load in loads:
        load.start()

    barrier = pltpu.get_barrier_semaphore()
    partners = [along(axis, step) for axis in "xz" for step in (1, 2, 3)] + [mirror, after, before]
    for partner in partners:
        pl.semaphore_signal(barrier, inc=1, device_id=partner, device_id_type=MESH)
    pl.semaphore_wait(barrier, len(partners))

    def send(source, target, send_sem, recv_sem, device_id):
        pltpu.make_async_remote_copy(
            src_ref=source, dst_ref=target, send_sem=send_sem, recv_sem=recv_sem,
            device_id=device_id, device_id_type=MESH,
        ).start()

    def arrived(like, recv_sem):
        pltpu.make_async_remote_copy(
            src_ref=like, dst_ref=like, send_sem=recv_sem, recv_sem=recv_sem,
            device_id=mirror, device_id_type=MESH,
        ).wait_recv()

    def departed(like, send_sem):
        pltpu.make_async_remote_copy(
            src_ref=like, dst_ref=like, send_sem=send_sem, recv_sem=send_sem,
            device_id=mirror, device_id_type=MESH,
        ).wait_send()

    blocks = {2: from_prev.at[0, 0, 0:2], 4: from_prev.at[0, 0], 6: scattered.at[0], 8: from_prev.at[0], 16: from_prev.at[0:2], 24: from_prev.at[0:3]}

    inner, outer = ("x", "z"), ("z", "x")
    low, high, whole = pl.ds(0, half), pl.ds(half, half), pl.ds(0, width)

    def slab(ref, index, h, step, lanes):
        at = (place[outer[h]] + step) % RING
        return ref.at[index, h, at, :, :, lanes] if h == 0 else ref.at[index, h, :, at, :, lanes]

    def block(ref, index, h, step):
        at = dict(place)
        at[inner[h]] = (place[inner[h]] + step) % RING
        return ref.at[index, h, at["z"], at["x"]]

    def gather_inner(a):
        for step in (1, 3) if a in PASSED else (1, 3, 2):
            for h in range(2):
                own = block(gathered, a, h, 0)
                send(own, own, ag_send.at[a, 0], ag_recv.at[a, 0], along(inner[h], step))

    def gather_pass(a):
        arrived(blocks[4], ag_recv.at[a, 0])
        for h in range(2):
            for step, lanes in ((1, low), (-1, high)):
                passed = block(gathered, a, h, -step).at[:, lanes]
                send(passed, passed, ag_send.at[a, 0], ag_recv.at[a, 3], along(inner[h], step))

    def gather_outer(a):
        if a in PASSED:
            arrived(blocks[2], ag_recv.at[a, 3])
        else:
            arrived(blocks[6], ag_recv.at[a, 0])
        for n, group in ((1, ((1, low), (-1, high))), (2, ((1, high), (-1, low)))):
            for h in range(2):
                for step, lanes in group:
                    own = slab(gathered, a, h, 0, lanes)
                    send(own, own, ag_send.at[a, 1], ag_recv.at[a, n], along(outer[h], step))

    def gather_relay(a):
        arrived(blocks[8], ag_recv.at[a, 1])
        for h in range(2):
            for step, lanes in ((1, low), (-1, high)):
                passed = slab(gathered, a, h, -step, lanes)
                send(passed, passed, ag_send.at[a, 1], ag_recv.at[a, 2], along(outer[h], step))

    def gather_end(a):
        arrived(blocks[16], ag_recv.at[a, 2])

    def scatter_start(p, h):
        for n, step, lanes, target, to in (
            (0, 2, low, pass_on, 1),
            (0, 2, high, pass_on, -1),
            (1, 1, high, from_prev, 1),
            (1, -1, low, from_next, -1),
        ):
            send(
                slab(partial, p, h, step, lanes), target.at[p, h, :, :, lanes],
                rs_send.at[p, 1], rs_recv.at[p, n], along(outer[h], to),
            )

    def scatter_relay(p):
        arrived(blocks[8], rs_recv.at[p, 0])
        for h in range(2):
            for step, lanes, target in ((1, low, from_prev), (-1, high, from_next)):
                mine = slab(partial, p, h, step, lanes)
                passing = pass_on[p, h, :, :, lanes].astype(F32)
                mine[...] = (mine[...].astype(F32) + passing).astype(BF16)
                send(
                    mine, target.at[p, h, :, :, lanes],
                    rs_send.at[p, 1], rs_recv.at[p, 1], along(outer[h], step),
                )

    def scatter_inner(p):
        arrived(blocks[16], rs_recv.at[p, 1])
        for h in range(2):
            total = slab(partial, p, h, 0, whole)[...].astype(F32)
            total = total + from_prev[p, h].astype(F32) + from_next[p, h].astype(F32)
            summed[p, h] = total.astype(BF16)
            for step in (1, 3, 2):
                at = (place[inner[h]] + step) % RING
                send(
                    summed.at[p, h, at], scattered.at[p, h, step - 1],
                    rs_send.at[p, 0], rs_recv.at[p, 2], along(inner[h], step),
                )

    def scatter_end(p):
        arrived(blocks[6], rs_recv.at[p, 2])
        halves = []
        for h in range(2):
            total = summed[p, h, pl.ds(place[inner[h]], 1)][0].astype(F32)
            for step in (1, 2, 3):
                total = total + scattered[p, h, step - 1].astype(F32)
            halves.append(total)
        return jnp.concatenate(halves, axis=1)

    def put_block(a, value):
        value = value.astype(BF16)
        for h in range(2):
            block(gathered, a, h, 0)[...] = value[:, h * width : (h + 1) * width]

    def factor_of(value):
        return lax.rsqrt(mean(value * value) + EPSILON)

    def normed(value):
        return value * factor_of(value) * gain

    def tokens(a, h):
        return gathered[a, h].reshape(RING * RING * 16, width)

    def onto_units(a, weights):
        return contract_last(tokens(a, 0), weights[0]) + contract_last(tokens(a, 1), weights[1])

    def onto_features(p, h, value, weights):
        tile = 256
        for n in range(width // tile):
            lanes = pl.ds(n * tile, tile)
            product = jnp.dot(value, weights[h, :, lanes], preferred_element_type=F32)
            partial[p, h, :, :, :, lanes] = product.astype(BF16).reshape(RING, RING, 16, tile)
        scatter_start(p, h)

    loaded = set()

    def weights_of(n):
        if n not in loaded:
            loaded.add(n)
            for load in loads[2 * n : 2 * n + 2]:
                load.wait()
        return (up, down)[n]

    def pairs(value):
        return value.reshape(RING * RING, 2, 8, units)

    def hidden_near(direction):
        gather_end(direction)
        hidden = pairs(onto_units(direction, weights_of(0)))
        for n in range(2):
            near[n, :, direction] = hidden[:, n]

    def hidden_forward(period):
        if period == 0:
            hidden = near[0].reshape(-1, units)
        else:
            gather_end(FB)
            hidden = onto_units(FB, weights_of(0))
        active[...] = (hidden * jax.nn.sigmoid(hidden)).astype(BF16)

    def hidden_backward(period):
        if period == 0:
            hidden = near[1].reshape(-1, units)
        else:
            gather_end(NB)
            hidden = onto_units(NB, weights_of(0))
        gating = jax.nn.sigmoid(hidden)
        flipped[3 + period] = (hidden * gating).astype(BF16).T
        bent[period] = gating * (1.0 + hidden * (1.0 - gating))

    def slope(period):
        gather_end(GS[period])
        slopes[period] = (onto_units(GS[period], weights_of(1)) * bent[period]).astype(BF16)

    def keep_slope(period):
        if period == 1:
            flipped[2] = slopes[1].T
            return
        value = pairs(wide(slopes[0]))
        for direction in range(2):
            mine = value[:, direction]
            mine = jnp.stack([jnp.zeros_like(mine), mine], axis=1).reshape(-1, units)
            flipped[direction] = mine.astype(BF16).T

    def weight_grad(first, arrays, h, target):
        tile = 256
        left = jnp.concatenate([flipped[first + n] for n in range(len(arrays))], axis=1)
        for n in range(width // tile):
            lanes = pl.ds(n * tile, tile)
            right = jnp.concatenate(
                [gathered[a, h, :, :, :, lanes].reshape(-1, tile) for a in arrays], axis=0
            )
            total = jnp.dot(left, right, preferred_element_type=F32)
            target[0, :, pl.ds(h * width + n * tile, tile)] = total.astype(BF16)

    def wide(value):
        return value.astype(F32)

    def folded(value):
        return jnp.concatenate([wide(value)[:, :width], wide(value)[:, width:]], axis=0).astype(BF16)

    def unfolded(value):
        return jnp.concatenate([wide(value)[:8], wide(value)[8:]], axis=1)

    def far_send_one(n, value):
        far_out[n] = folded(value)
        send(far_out.at[n], far_in.at[n], far_send.at[0], far_recv.at[n], mirror)

    def from_far(n):
        arrived(far_in.at[n], far_recv.at[n])
        return unfolded(far_in[n])

    def with_far(own, n):
        return jnp.concatenate([wide(own), from_far(n)], axis=0)

    def hop(n, value, to):
        hop_out[n] = value
        send(hop_out.at[n], hop_in.at[n], hop_send.at[0], hop_recv.at[n], to)

    def hopped(n):
        arrived(hop_in.at[n], hop_recv.at[n])
        return wide(hop_in[n])

    def deliver(n, target, period, value):
        mirror_out[n] = folded(value[8:])
        send(mirror_out.at[n], mirror_in.at[n], mirror_send.at[0], mirror_recv.at[n], mirror)
        target[period, 0, 0] = value[:8].astype(BF16)

    def delivered(n, target, period):
        arrived(mirror_in.at[n], mirror_recv.at[n])
        target[period, 1, 0] = unfolded(mirror_in[n]).astype(BF16)

    def rounded(value):
        return wide(value.astype(BF16))

    def finish_forward(period):
        p = 2 * period
        produced = rounded(rows[FS[period]] + scatter_end(p))
        if period == 0:
            hop(0, produced.astype(BF16), after)
        deliver(p, states_out, period, produced)

    def finish_backward(period):
        p = 2 * period + 1
        scaled = scatter_end(p) * gain
        own = rows[NS[period]]
        factor = factor_of(own)
        unit = own * factor
        back = factor * (scaled - unit * mean(unit * scaled))
        back = rounded(rows[GS[period]] + back)
        if period == 0:
            hop(1, back.astype(BF16), before)
        deliver(p, input_grads, period, back)

    def begin(a, value):
        rows[a] = value
        put_block(a, value if a in GS else normed(value))
        gather_inner(a)

    def begin_near(direction, forward, kept):
        own = pl.ds(8 * direction, 8)
        rows[NEAR_FORWARD, own] = forward
        rows[NEAR_SAVED, own] = kept
        put_block(direction, normed(jnp.concatenate([forward, kept], axis=0)))
        gather_inner(direction)

    def joined(pair):
        return jnp.concatenate([wide(pair[0]), wide(pair[1])], axis=0)

    def begin_later_forward():
        begin(FB, jnp.where(s == 0, joined(entering[0]), hopped(0)))

    def begin_later_grads():
        begin(GB, jnp.where(s == sections - 1, joined(cot_entering[0]), hopped(1)))

    def far_rest():
        far_send_one(2, cotangent[1, 0])
        far_send_one(3, saved[1, 1, 0])

    def end():
        for n, target in enumerate((states_out, input_grads) * 2):
            delivered(n, target, n // 2)
        for like, sem in ((far_out, far_send), (hop_out, hop_send), (mirror_out, mirror_send)):
            departed(like, sem.at[0])
        for sem, count in ((ag_send, 6), (rs_send, 4)):
            for n in range(count):
                departed(blocks[6], sem.at[n, 0])
                departed(blocks[24], sem.at[n, 1])

    chosen = lax.broadcasted_iota(jnp.int32, gains.shape, 0) == s
    gain = jnp.sum(jnp.where(chosen, wide(gains[...]), 0.0), axis=0, keepdims=True)
    steps = {
        "far0": lambda: far_send_one(0, states_in[1, 0]),
        "far1": lambda: far_send_one(1, saved[0, 1, 0]),
        "far2": far_rest,
        "nD0": lambda: begin_near(D0, wide(states_in[0, 0]), wide(saved[0, 0, 0])),
        "nD1": lambda: begin_near(D1, from_far(0), from_far(1)),
        "nG0": lambda: begin(GA, with_far(cotangent[0, 0], 2)),
        "nN1": lambda: begin(NB, with_far(saved[1, 0, 0], 3)),
        "hD0": lambda: hidden_near(D0),
        "hD1": lambda: hidden_near(D1),
        "nF1": begin_later_forward,
        "nG1": begin_later_grads,
        "w1a": lambda: weight_grad(3, (GA, GB), 0, grad_down),
        "w1b": lambda: weight_grad(3, (GA, GB), 1, grad_down),
        "w0a": lambda: weight_grad(0, (D0, D1, NB), 0, grad_up),
        "w0b": lambda: weight_grad(0, (D0, D1, NB), 1, grad_up),
        "end": end,
    }
    for a, name in enumerate(("D0", "D1", "G0", "N1", "F1", "G1")):
        steps["ir" + name] = functools.partial(gather_pass, a)
        steps["out" + name] = functools.partial(gather_outer, a)
        steps["rel" + name] = functools.partial(gather_relay, a)
    for period in range(2):
        k = str(period)
        steps["hF" + k] = functools.partial(hidden_forward, period)
        steps["hB" + k] = functools.partial(hidden_backward, period)
        steps["gB" + k] = functools.partial(slope, period)
        steps["keepB" + k] = functools.partial(keep_slope, period)
        steps["finF" + k] = functools.partial(finish_forward, period)
        steps["finB" + k] = functools.partial(finish_backward, period)
        for h in range(2):
            steps[f"pF{k}h{h}"] = lambda p=2 * period, h=h: onto_features(p, h, active[...], weights_of(1))
            steps[f"pB{k}h{h}"] = lambda p=2 * period + 1, h=h: onto_features(
                p, h, slopes[p // 2], weights_of(0)
            )
        for n, name in enumerate("FB"):
            steps["rsr" + name + k] = functools.partial(scatter_relay, 2 * period + n)
            steps["rsi" + name + k] = functools.partial(scatter_inner, 2 * period + n)
    for name in ORDER:
        steps[name]()


def write_out(*refs):
    sems = refs[-1]
    copies = [pltpu.make_async_copy(refs[n], refs[4 + n], sems.at[n]) for n in range(4)]
    for copy in copies:
        copy.start()
    for copy in copies:
        copy.wait()


def body(states_in, entering, saved, cotangent, cot_entering, gains, up_rows, down_rows):
    units, features = up_rows.shape[2:]
    width = features // 2
    dma, vmem = pltpu.SemaphoreType.DMA, pltpu.VMEM
    in_vmem = pl.BlockSpec(memory_space=pltpu.VMEM)
    anywhere = pl.BlockSpec(memory_space=pl.ANY)
    grid_rows = (RING, RING, 16, width)
    shapes = (saved.shape, saved.shape, (1, units, features), (1, units, features))
    results = pl.pallas_call(
        kernel,
        out_shape=tuple(vmem(shape, BF16) for shape in shapes),
        in_specs=[in_vmem] * 6 + [anywhere] * 2,
        out_specs=(in_vmem,) * 4,
        scratch_shapes=[
            vmem((2, units, width), BF16),
            vmem((2, units, width), BF16),
            vmem((6, 2) + grid_rows, BF16),
            vmem((4, 2) + grid_rows, BF16),
            vmem((4, 2) + grid_rows[1:], BF16),
            vmem((4, 2) + grid_rows[1:], BF16),
            vmem((4, 2) + grid_rows[1:], BF16),
            vmem((4, 2) + grid_rows[1:], BF16),
            vmem((4, 2, 3, 16, width), BF16),
            vmem((6, 16, features), F32),
            vmem((4, 16, width), BF16),
            vmem((4, 16, width), BF16),
            vmem((2, 16, features), BF16),
            vmem((2, 16, features), BF16),
            vmem((4, 16, width), BF16),
            vmem((4, 16, width), BF16),
            vmem((2, 256, units), BF16),
            vmem((2, 256, units), F32),
            vmem((256, units), BF16),
            vmem((5, units, 256), BF16),
            vmem((2, 16, 2, 8, units), F32),
            dma((4,)),
            dma((6, 2)),
            dma((6, 4)),
            dma((4, 2)),
            dma((4, 3)),
            dma((1,)),
            dma((4,)),
            dma((1,)),
            dma((2,)),
            dma((1,)),
            dma((4,)),
        ],
        compiler_params=pltpu.CompilerParams(
            collective_id=0, has_side_effects=True, vmem_limit_bytes=48 * 2**20
        ),
        cost_estimate=pl.CostEstimate(flops=15 * 10**9, bytes_accessed=17 * 10**6, transcendentals=0),
    )(states_in, entering, saved, cotangent, cot_entering, gains, up_rows, down_rows)
    return pl.pallas_call(
        write_out,
        out_shape=tuple(jax.ShapeDtypeStruct(shape, BF16) for shape in shapes),
        in_specs=[in_vmem] * 4,
        out_specs=(anywhere,) * 4,
        scratch_shapes=[dma((4,))],
        compiler_params=pltpu.CompilerParams(vmem_limit_bytes=4 * 2**20),
    )(*results)


def solution(mesh):
    group = ("dp", "tensor")
    placed = (
        P(None, "section", group, None),
        P(None, None, group, None),
        P(None, None, "section", group, None),
        P(None, "section", group, None),
        P(None, None, group, None),
        P(),
        P("section", None, group, None),
        P("section", None, group, None),
    )
    return jax.shard_map(
        body,
        mesh=mesh,
        in_specs=placed,
        out_specs=(
            P(None, None, "section", group, None),
            P(None, None, "section", group, None),
            P("section", group, None),
            P("section", group, None),
        ),
        check_vma=False,
    )
```

```python
import functools

import jax
import jax.numpy as jnp
from jax import lax
from jax.experimental import pallas as pl
from jax.experimental.pallas import tpu as pltpu
from jax.sharding import PartitionSpec as P

EPSILON = 1e-06
MESH = pl.DeviceIdType.MESH
F32, BF16 = jnp.float32, jnp.bfloat16
D0, D1, GA, NB, FB, GB = range(6)
NEAR_FORWARD, NEAR_SAVED = 0, 1
FS, NS, GS = (NEAR_FORWARD, FB), (NEAR_SAVED, NB), (GA, GB)
PASSED = (GA, NB, D1, GB,)
RING = 4

ORDER = (
    "far0", "far1", "far2", "nD0", "nD1", "outD0", "nG0", "irD1", "relD0", "irG0", "outD1",
    "relD1", "outG0", "hD0", "hD1", "hF0", "relG0", "pF0h0", "pF0h1", "hB0", "nN1", "gB0", "rsrF0",
    "pB0h0", "pB0h1", "rsrB0", "rsiF0", "irN1", "rsiB0", "finF0", "outN1", "finB0", "nF1", "relN1",
    "nG1", "keepB0", "outF1", "hB1", "irG1", "relF1", "outG1", "hF1", "relG1", "pF1h0", "pF1h1",
    "gB1", "pB1h0", "pB1h1", "keepB1", "w0a", "rsrF1", "rsrB1", "w1a", "w1b", "rsiF1", "rsiB1",
    "w0b", "finF1", "finB1", "end",
)


def contract_last(former, latter):
    return lax.dot_general(former, latter, (((1,), (1,)), ((), ())), preferred_element_type=F32)


def mean(value):
    return jnp.mean(value, axis=-1, keepdims=True)


def kernel(
    states_in, entering, saved, cotangent, cot_entering, gains, up_rows, down_rows,
    states_out, input_grads, grad_up, grad_down,
    up, down, gathered, partial, pass_on, from_prev, from_next, summed, scattered,
    split_out, split_in, rows, far_out, far_in, hop_out, hop_in, landed, mirror_out, mirror_in,
    slopes, bent, active, flipped, near,
    load_sem, ag_send, ag_recv, rs_send, rs_recv, far_send, far_recv,
    hop_send, hop_recv, mirror_send, mirror_recv,
):
    s = lax.axis_index("section")
    d = lax.axis_index("dp")
    t = lax.axis_index("tensor")
    sections = lax.axis_size("section")
    width = up.shape[-1]
    half = width // 2
    features = 2 * width
    units = up.shape[1]
    place = {"x": d % RING, "z": (d // RING) * 2 + t}

    far = sections - 1 - s

    def device(section, x, z):
        return (section, (z // 2) * RING + x, z % 2)

    def moved(section, axis, step):
        to = dict(place)
        to[axis] = (place[axis] + step) % RING
        return device(section, to["x"], to["z"])

    steps_away = [(axis, step) for axis in "xz" for step in (1, 2, 3)]
    neighbours = {away: moved(s, *away) for away in steps_away}
    far_neighbours = {away: moved(far, *away) for away in steps_away}
    mirror = device(far, place["x"], place["z"])

    def along(axis, step):
        return neighbours[axis, step % RING]

    def far_along(axis, step):
        return far_neighbours[axis, step] if step else mirror

    after = device((s + 1) % sections, place["x"], place["z"])
    before = device((s + sections - 1) % sections, place["x"], place["z"])

    loads = [
        pltpu.make_async_copy(
            source.at[0, 0, :, pl.ds(h * width, width)], target.at[h], load_sem.at[2 * n + h]
        )
        for n, (source, target) in enumerate(((up_rows, up), (down_rows, down)))
        for h in range(2)
    ]
    for load in loads:
        load.start()

    barrier = pltpu.get_barrier_semaphore()
    partners = list(neighbours.values()) + list(far_neighbours.values()) + [mirror, after, before]
    for partner in partners:
        pl.semaphore_signal(barrier, inc=1, device_id=partner, device_id_type=MESH)
    def send(source, target, send_sem, recv_sem, device_id):
        pltpu.make_async_remote_copy(
            src_ref=source, dst_ref=target, send_sem=send_sem, recv_sem=recv_sem,
            device_id=device_id, device_id_type=MESH,
        ).start()

    def arrived(like, recv_sem):
        pltpu.make_async_remote_copy(
            src_ref=like, dst_ref=like, send_sem=recv_sem, recv_sem=recv_sem,
            device_id=mirror, device_id_type=MESH,
        ).wait_recv()

    def departed(like, send_sem):
        pltpu.make_async_remote_copy(
            src_ref=like, dst_ref=like, send_sem=send_sem, recv_sem=send_sem,
            device_id=mirror, device_id_type=MESH,
        ).wait_send()

    blocks = {2: from_prev.at[0, 0, 0:2], 4: from_prev.at[0, 0], 6: scattered.at[0], 8: from_prev.at[0], 16: from_prev.at[0:2], 24: from_prev.at[0:3]}

    inner, outer = ("x", "z"), ("z", "x")
    low, high, whole = pl.ds(0, half), pl.ds(half, half), pl.ds(0, width)

    def slab(ref, index, h, step, lanes):
        at = (place[outer[h]] + step) % RING
        return ref.at[index, h, at, :, :, lanes] if h == 0 else ref.at[index, h, :, at, :, lanes]

    def block(ref, index, h, step):
        at = dict(place)
        at[inner[h]] = (place[inner[h]] + step) % RING
        return ref.at[index, h, at["z"], at["x"]]

    def gather_inner(a):
        for step in (1, 3) if a in PASSED else (1, 3, 2):
            for h in range(2):
                own = block(gathered, a, h, 0)
                send(own, own, ag_send.at[a, 0], ag_recv.at[a, 0], along(inner[h], step))

    def gather_pass(a):
        arrived(blocks[4], ag_recv.at[a, 0])
        for h in range(2):
            for step, lanes in ((1, low), (-1, high)):
                passed = block(gathered, a, h, -step).at[:, lanes]
                send(passed, passed, ag_send.at[a, 0], ag_recv.at[a, 3], along(inner[h], step))

    def gather_outer(a):
        if a in PASSED:
            arrived(blocks[2], ag_recv.at[a, 3])
        else:
            arrived(blocks[6], ag_recv.at[a, 0])
        for n, group in ((1, ((1, low), (-1, high))), (2, ((1, high), (-1, low)))):
            for h in range(2):
                for step, lanes in group:
                    own = slab(gathered, a, h, 0, lanes)
                    send(own, own, ag_send.at[a, 1], ag_recv.at[a, n], along(outer[h], step))

    def gather_relay(a):
        arrived(blocks[8], ag_recv.at[a, 1])
        for h in range(2):
            for step, lanes in ((1, low), (-1, high)):
                passed = slab(gathered, a, h, -step, lanes)
                send(passed, passed, ag_send.at[a, 1], ag_recv.at[a, 2], along(outer[h], step))

    def gather_end(a):
        arrived(blocks[16], ag_recv.at[a, 2])

    def scatter_start(p, h):
        for n, step, lanes, target, to in (
            (0, 2, low, pass_on, 1),
            (0, 2, high, pass_on, -1),
            (1, 1, high, from_prev, 1),
            (1, -1, low, from_next, -1),
        ):
            send(
                slab(partial, p, h, step, lanes), target.at[p, h, :, :, lanes],
                rs_send.at[p, 1], rs_recv.at[p, n], along(outer[h], to),
            )

    def scatter_relay(p):
        arrived(blocks[8], rs_recv.at[p, 0])
        for h in range(2):
            for step, lanes, target in ((1, low, from_prev), (-1, high, from_next)):
                mine = slab(partial, p, h, step, lanes)
                passing = pass_on[p, h, :, :, lanes].astype(F32)
                mine[...] = (mine[...].astype(F32) + passing).astype(BF16)
                send(
                    mine, target.at[p, h, :, :, lanes],
                    rs_send.at[p, 1], rs_recv.at[p, 1], along(outer[h], step),
                )

    def scatter_out(p):
        arrived(blocks[16], rs_recv.at[p, 1])
        for h in range(2):
            total = slab(partial, p, h, 0, whole)[...].astype(F32)
            total = total + from_prev[p, h].astype(F32) + from_next[p, h].astype(F32)
            total = total.reshape(RING, 2, 8, width)
            for direction in range(2):
                part = total[:, direction]
                part = jnp.concatenate([part[:, :, :half], part[:, :, half:]], axis=1)
                split_out[p % 2, h, direction] = part.astype(BF16)
            for step in (1, 3, 2, 0):
                at = (place[inner[h]] + step) % RING
                sems = (rs_send.at[p, 0], rs_recv.at[p, 2])
                for direction in range(2):
                    if direction or step:
                        to = far_along(inner[h], step) if direction else along(inner[h], step)
                        slot = 3 + step if direction else step - 1
                        send(split_out.at[p % 2, h, direction, at], split_in.at[p % 2, h, slot], *sems, to)

    def scatter_in(p):
        arrived(split_in.at[0], rs_recv.at[p, 2])
        sums = []
        for direction in range(2):
            halves = []
            for h in range(2):
                parts = [split_in[p % 2, h, slot] for slot in (range(3, 7) if direction else range(3))]
                if not direction:
                    parts.append(split_out[p % 2, h, 0, pl.ds(place[inner[h]], 1)][0])
                total = sum(part.astype(F32) for part in parts)
                halves += [total[:8], total[8:]]
            sums.append(jnp.concatenate(halves, axis=1))
        return sums

    def scatter_inner(p):
        if p >= 2:
            return scatter_out(p)
        arrived(blocks[16], rs_recv.at[p, 1])
        for h in range(2):
            total = slab(partial, p, h, 0, whole)[...].astype(F32)
            total = total + from_prev[p, h].astype(F32) + from_next[p, h].astype(F32)
            summed[p, h] = total.astype(BF16)
            for step in (1, 3, 2):
                at = (place[inner[h]] + step) % RING
                send(
                    summed.at[p, h, at], scattered.at[p, h, step - 1],
                    rs_send.at[p, 0], rs_recv.at[p, 2], along(inner[h], step),
                )

    def scatter_end(p):
        arrived(blocks[6], rs_recv.at[p, 2])
        halves = []
        for h in range(2):
            total = summed[p, h, pl.ds(place[inner[h]], 1)][0].astype(F32)
            for step in (1, 2, 3):
                total = total + scattered[p, h, step - 1].astype(F32)
            halves.append(total)
        return jnp.concatenate(halves, axis=1)

    def put_block(a, value):
        value = value.astype(BF16)
        for h in range(2):
            block(gathered, a, h, 0)[...] = value[:, h * width : (h + 1) * width]

    def factor_of(value):
        return lax.rsqrt(mean(value * value) + EPSILON)

    def normed(value):
        return value * factor_of(value) * gain

    def norm_back(own, upstream, scaling, d_normed):
        scaled = d_normed * scaling
        factor = factor_of(own)
        unit = own * factor
        return upstream + factor * (scaled - unit * mean(unit * scaled))

    def tokens(a, h):
        return gathered[a, h].reshape(RING * RING * 16, width)

    def onto_units(a, weights):
        return contract_last(tokens(a, 0), weights[0]) + contract_last(tokens(a, 1), weights[1])

    def onto_features(p, h, value, weights):
        tile = 256
        for n in range(width // tile):
            lanes = pl.ds(n * tile, tile)
            product = jnp.dot(value, weights[h, :, lanes], preferred_element_type=F32)
            partial[p, h, :, :, :, lanes] = product.astype(BF16).reshape(RING, RING, 16, tile)
        scatter_start(p, h)

    loaded = set()

    def weights_of(n):
        if n not in loaded:
            loaded.add(n)
            for load in loads[2 * n : 2 * n + 2]:
                load.wait()
        return (up, down)[n]

    def pairs(value):
        return value.reshape(RING * RING, 2, 8, units)

    def hidden_near(direction):
        gather_end(direction)
        hidden = pairs(onto_units(direction, weights_of(0)))
        for n in range(2):
            near[n, :, direction] = hidden[:, n]

    def hidden_forward(period):
        if period == 0:
            hidden = near[0].reshape(-1, units)
        else:
            gather_end(FB)
            hidden = onto_units(FB, weights_of(0))
        active[...] = (hidden * jax.nn.sigmoid(hidden)).astype(BF16)

    def hidden_backward(period):
        if period == 0:
            hidden = near[1].reshape(-1, units)
        else:
            gather_end(NB)
            hidden = onto_units(NB, weights_of(0))
        gating = jax.nn.sigmoid(hidden)
        flipped[3 + period] = (hidden * gating).astype(BF16).T
        bent[period] = gating * (1.0 + hidden * (1.0 - gating))

    def slope(period):
        gather_end(GS[period])
        slopes[period] = (onto_units(GS[period], weights_of(1)) * bent[period]).astype(BF16)

    def keep_slope(period):
        if period == 1:
            flipped[2] = slopes[1].T
            return
        value = pairs(wide(slopes[0]))
        for direction in range(2):
            mine = value[:, direction]
            mine = jnp.stack([jnp.zeros_like(mine), mine], axis=1).reshape(-1, units)
            flipped[direction] = mine.astype(BF16).T

    def weight_grad(first, arrays, h, target):
        tile = 256
        left = jnp.concatenate([flipped[first + n] for n in range(len(arrays))], axis=1)
        for n in range(width // tile):
            lanes = pl.ds(n * tile, tile)
            right = jnp.concatenate(
                [gathered[a, h, :, :, :, lanes].reshape(-1, tile) for a in arrays], axis=0
            )
            total = jnp.dot(left, right, preferred_element_type=F32)
            target[0, :, pl.ds(h * width + n * tile, tile)] = total.astype(BF16)

    def wide(value):
        return value.astype(F32)

    def folded(value):
        return jnp.concatenate([wide(value)[:, :width], wide(value)[:, width:]], axis=0).astype(BF16)

    def unfolded(value):
        return jnp.concatenate([wide(value)[:8], wide(value)[8:]], axis=1)

    def far_ready(n):
        send(far_out.at[n], far_in.at[n], far_send.at[0], far_recv.at[n], mirror)

    def far_send_one(n, value):
        far_out[n] = folded(value)
        far_ready(n)

    def from_far(n):
        arrived(far_in.at[n], far_recv.at[n])
        return unfolded(far_in[n])

    def with_far(own, n):
        return jnp.concatenate([wide(own), from_far(n)], axis=0)

    def hop(n, value, to):
        hop_out[n] = value

        @pl.when(s != (0 if n else sections - 1))
        def _():
            send(hop_out.at[n], hop_in.at[n], hop_send.at[n], hop_recv.at[n], to)

    def hopped(n, entered, edge):
        @pl.when(s == edge)
        def _():
            landed[...] = joined(entered[0])

        @pl.when(s != edge)
        def _():
            arrived(hop_in.at[n], hop_recv.at[n])
            landed[...] = wide(hop_in[n])

        return landed[...]

    def deliver(n, target, period, value):
        mirror_out[n] = folded(value[8:])
        send(mirror_out.at[n], mirror_in.at[n], mirror_send.at[0], mirror_recv.at[n], mirror)
        target[period, 0, 0] = value[:8].astype(BF16)

    def delivered(n, target, period):
        arrived(mirror_in.at[n], mirror_recv.at[n])
        target[period, 1, 0] = unfolded(mirror_in[n]).astype(BF16)

    def rounded(value):
        return wide(value.astype(BF16))

    def finish_forward(period):
        if period == 1:
            near_sum, far_sum = scatter_in(2)
            states_out[1, 0, 0] = (rows[FB, 0:8] + near_sum).astype(BF16)
            states_out[1, 1, 0] = (from_far(4) + far_sum).astype(BF16)
            return
        produced = rounded(rows[NEAR_FORWARD] + scatter_end(0))
        hop(0, produced.astype(BF16), after)
        deliver(0, states_out, 0, produced)

    def finish_backward(period):
        if period == 1:
            near_sum, far_sum = scatter_in(3)
            back = norm_back(rows[NB, 0:8], rows[GB, 0:8], gain, near_sum)
            input_grads[1, 0, 0] = back.astype(BF16)
            back = norm_back(wide(saved[1, 1, 0]), from_far(5), far_gain, far_sum)
            input_grads[1, 1, 0] = back.astype(BF16)
            return
        back = rounded(norm_back(rows[NEAR_SAVED], rows[GA], gain, scatter_end(1)))
        hop(1, back.astype(BF16), before)
        deliver(1, input_grads, 0, back)

    def begin(a, value):
        rows[a] = value
        put_block(a, value if a in GS else normed(value))
        gather_inner(a)

    def begin_near(direction, forward, kept):
        own = pl.ds(8 * direction, 8)
        rows[NEAR_FORWARD, own] = forward
        rows[NEAR_SAVED, own] = kept
        put_block(direction, normed(jnp.concatenate([forward, kept], axis=0)))

    def joined(pair):
        return jnp.concatenate([wide(pair[0]), wide(pair[1])], axis=0)

    def begin_later_forward():
        begin(FB, hopped(0, entering, 0))
        far_send_one(4, rows[FB, 8:16])

    def begin_later_grads():
        begin(GB, hopped(1, cot_entering, sections - 1))
        far_send_one(5, rows[GB, 8:16])

    def begin_far():
        begin_near(D1, from_far(0), from_far(1))
        gather_inner(D1)

    def far_rest():
        far_ready(2)
        far_ready(3)

    def end():
        delivered(0, states_out, 0)
        delivered(1, input_grads, 0)
        for like, sem in ((far_out, far_send), (mirror_out, mirror_send)):
            departed(like, sem.at[0])

        @pl.when(s != sections - 1)
        def _():
            departed(hop_out.at[0], hop_send.at[0])

        @pl.when(s != 0)
        def _():
            departed(hop_out.at[1], hop_send.at[1])

        for sem, count in ((ag_send, 6), (rs_send, 4)):
            for n in range(count):
                departed(split_in.at[0] if sem is rs_send and n >= 2 else blocks[6], sem.at[n, 0])
                departed(blocks[24], sem.at[n, 1])

    def gain_of(layer):
        chosen = lax.broadcasted_iota(jnp.int32, gains.shape, 0) == layer
        return jnp.sum(jnp.where(chosen, wide(gains[...]), 0.0), axis=0, keepdims=True)

    gain, far_gain = gain_of(s), gain_of(far)
    steps = {
        "far0": lambda: far_ready(0),
        "far1": lambda: far_ready(1),
        "far2": far_rest,
        "nD0": lambda: gather_inner(D0),
        "nD1": begin_far,
        "nG0": lambda: begin(GA, with_far(cotangent[0, 0], 2)),
        "nN1": lambda: begin(NB, with_far(saved[1, 0, 0], 3)),
        "hD0": lambda: hidden_near(D0),
        "hD1": lambda: hidden_near(D1),
        "nF1": begin_later_forward,
        "nG1": begin_later_grads,
        "w1a": lambda: weight_grad(3, (GA, GB), 0, grad_down),
        "w1b": lambda: weight_grad(3, (GA, GB), 1, grad_down),
        "w0a": lambda: weight_grad(0, (D0, D1, NB), 0, grad_up),
        "w0b": lambda: weight_grad(0, (D0, D1, NB), 1, grad_up),
        "end": end,
    }
    for a, name in enumerate(("D0", "D1", "G0", "N1", "F1", "G1")):
        steps["ir" + name] = functools.partial(gather_pass, a)
        steps["out" + name] = functools.partial(gather_outer, a)
        steps["rel" + name] = functools.partial(gather_relay, a)
    for period in range(2):
        k = str(period)
        steps["hF" + k] = functools.partial(hidden_forward, period)
        steps["hB" + k] = functools.partial(hidden_backward, period)
        steps["gB" + k] = functools.partial(slope, period)
        steps["keepB" + k] = functools.partial(keep_slope, period)
        steps["finF" + k] = functools.partial(finish_forward, period)
        steps["finB" + k] = functools.partial(finish_backward, period)
        for h in range(2):
            steps[f"pF{k}h{h}"] = lambda p=2 * period, h=h: onto_features(p, h, active[...], weights_of(1))
            steps[f"pB{k}h{h}"] = lambda p=2 * period + 1, h=h: onto_features(
                p, h, slopes[p // 2], weights_of(0)
            )
        for n, name in enumerate("FB"):
            steps["rsr" + name + k] = functools.partial(scatter_relay, 2 * period + n)
            steps["rsi" + name + k] = functools.partial(scatter_inner, 2 * period + n)
    for n, value in enumerate((states_in[1, 0], saved[0, 1, 0], cotangent[1, 0], saved[1, 1, 0])):
        far_out[n] = folded(value)
    begin_near(D0, wide(states_in[0, 0]), wide(saved[0, 0, 0]))
    pl.semaphore_wait(barrier, len(partners))
    for name in ORDER:
        steps[name]()


def write_out(*refs):
    sems = refs[-1]
    copies = [pltpu.make_async_copy(refs[n], refs[4 + n], sems.at[n]) for n in range(4)]
    for copy in copies:
        copy.start()
    for copy in copies:
        copy.wait()


def body(states_in, entering, saved, cotangent, cot_entering, gains, up_rows, down_rows):
    units, features = up_rows.shape[2:]
    width = features // 2
    dma, vmem = pltpu.SemaphoreType.DMA, pltpu.VMEM
    in_vmem = pl.BlockSpec(memory_space=pltpu.VMEM)
    anywhere = pl.BlockSpec(memory_space=pl.ANY)
    grid_rows = (RING, RING, 16, width)
    shapes = (saved.shape, saved.shape, (1, units, features), (1, units, features))
    results = pl.pallas_call(
        kernel,
        out_shape=tuple(vmem(shape, BF16) for shape in shapes),
        in_specs=[in_vmem] * 6 + [anywhere] * 2,
        out_specs=(in_vmem,) * 4,
        scratch_shapes=[
            vmem((2, units, width), BF16),
            vmem((2, units, width), BF16),
            vmem((6, 2) + grid_rows, BF16),
            vmem((4, 2) + grid_rows, BF16),
            vmem((4, 2) + grid_rows[1:], BF16),
            vmem((4, 2) + grid_rows[1:], BF16),
            vmem((4, 2) + grid_rows[1:], BF16),
            vmem((4, 2) + grid_rows[1:], BF16),
            vmem((4, 2, 3, 16, width), BF16),
            vmem((2, 2, 2, RING, 16, width // 2), BF16),
            vmem((2, 2, 7, 16, width // 2), BF16),
            vmem((6, 16, features), F32),
            vmem((6, 16, width), BF16),
            vmem((6, 16, width), BF16),
            vmem((2, 16, features), BF16),
            vmem((2, 16, features), BF16),
            vmem((16, features), F32),
            vmem((2, 16, width), BF16),
            vmem((2, 16, width), BF16),
            vmem((2, 256, units), BF16),
            vmem((2, 256, units), F32),
            vmem((256, units), BF16),
            vmem((5, units, 256), BF16),
            vmem((2, 16, 2, 8, units), F32),
            dma((4,)),
            dma((6, 2)),
            dma((6, 4)),
            dma((4, 2)),
            dma((4, 3)),
            dma((1,)),
            dma((6,)),
            dma((2,)),
            dma((2,)),
            dma((1,)),
            dma((2,)),
        ],
        compiler_params=pltpu.CompilerParams(
            collective_id=0, has_side_effects=True, vmem_limit_bytes=48 * 2**20
        ),
        cost_estimate=pl.CostEstimate(flops=15 * 10**9, bytes_accessed=17 * 10**6, transcendentals=0),
    )(states_in, entering, saved, cotangent, cot_entering, gains, up_rows, down_rows)
    return pl.pallas_call(
        write_out,
        out_shape=tuple(jax.ShapeDtypeStruct(shape, BF16) for shape in shapes),
        in_specs=[in_vmem] * 4,
        out_specs=(anywhere,) * 4,
        scratch_shapes=[dma((4,))],
        compiler_params=pltpu.CompilerParams(vmem_limit_bytes=4 * 2**20),
    )(*results)


def solution(mesh):
    group = ("dp", "tensor")
    placed = (
        P(None, "section", group, None),
        P(None, None, group, None),
        P(None, None, "section", group, None),
        P(None, "section", group, None),
        P(None, None, group, None),
        P(),
        P("section", None, group, None),
        P("section", None, group, None),
    )
    return jax.shard_map(
        body,
        mesh=mesh,
        in_specs=placed,
        out_specs=(
            P(None, None, "section", group, None),
            P(None, None, "section", group, None),
            P("section", group, None),
            P("section", group, None),
        ),
        check_vma=False,
    )
```

```python
import functools

import jax
import jax.numpy as jnp
from jax import lax
from jax.experimental import pallas as pl
from jax.experimental.pallas import tpu as pltpu
from jax.sharding import PartitionSpec as P

EPSILON = 1e-06
MESH = pl.DeviceIdType.MESH
F32, BF16 = jnp.float32, jnp.bfloat16
D0, D1, GA, NB, FB, GB = range(6)
NEAR_FORWARD, NEAR_SAVED = 0, 1
FS, NS, GS = (NEAR_FORWARD, FB), (NEAR_SAVED, NB), (GA, GB)
PASSED = (GA, NB, D1, GB,)
RING = 4

ORDER = (
    "far0", "far1", "far2", "nD0", "nD1", "outD0", "nG0", "irD1", "relD0", "irG0", "outD1",
    "relD1", "outG0", "hD0", "hD1", "hF0", "relG0", "pF0h0", "pF0h1", "hB0", "nN1", "gB0", "rsrF0",
    "pB0h0", "pB0h1", "rsrB0", "rsiF0", "irN1", "rsiB0", "finF0", "outN1", "finB0", "nF1", "relN1",
    "nG1", "keepB0", "outF1", "hB1", "irG1", "relF1", "outG1", "hF1", "relG1", "pF1h0", "pF1h1",
    "gB1", "pB1h0", "pB1h1", "keepB1", "w0a", "rsrF1", "rsrB1", "w1a", "w1b", "rsiF1", "rsiB1",
    "w0b", "finF1", "finB1", "end",
)


def contract_last(former, latter):
    return lax.dot_general(former, latter, (((1,), (1,)), ((), ())), preferred_element_type=F32)


def mean(value):
    return jnp.mean(value, axis=-1, keepdims=True)


def kernel(
    states_in_hbm, entering_hbm, saved_hbm, cotangent_hbm, cot_entering_hbm, gains_hbm, up_rows, down_rows,
    states_out, input_grads, grad_up, grad_down,
    up, down, gathered, partial, pass_on, from_prev, from_next, summed, scattered,
    split_out, split_in, rows, far_out, far_in, hop_out, hop_in, landed, mirror_out, mirror_in,
    slopes, bent, active, flipped, near,
    states_in, entering, saved, cotangent, cot_entering, gains, load_sem, small_sem, ag_send, ag_recv, rs_send, rs_recv, far_send, far_recv,
    hop_send, hop_recv, mirror_send, mirror_recv,
):
    s = lax.axis_index("section")
    d = lax.axis_index("dp")
    t = lax.axis_index("tensor")
    sections = lax.axis_size("section")
    width = up.shape[-1]
    half = width // 2
    features = 2 * width
    units = up.shape[1]
    place = {"x": d % RING, "z": (d // RING) * 2 + t}

    far = sections - 1 - s

    def device(section, x, z):
        return (section, (z // 2) * RING + x, z % 2)

    def moved(section, axis, step):
        to = dict(place)
        to[axis] = (place[axis] + step) % RING
        return device(section, to["x"], to["z"])

    steps_away = [(axis, step) for axis in "xz" for step in (1, 2, 3)]
    neighbours = {away: moved(s, *away) for away in steps_away}
    far_neighbours = {away: moved(far, *away) for away in steps_away}
    mirror = device(far, place["x"], place["z"])

    def along(axis, step):
        return neighbours[axis, step % RING]

    def far_along(axis, step):
        return far_neighbours[axis, step] if step else mirror

    after = device((s + 1) % sections, place["x"], place["z"])
    before = device((s + sections - 1) % sections, place["x"], place["z"])

    barrier = pltpu.get_barrier_semaphore()
    partners = list(neighbours.values()) + list(far_neighbours.values()) + [mirror, after, before]
    for partner in partners:
        pl.semaphore_signal(barrier, inc=1, device_id=partner, device_id_type=MESH)
    small = [
        pltpu.make_async_copy(source, target, small_sem.at[n])
        for n, (source, target) in enumerate((
            (states_in_hbm, states_in), (saved_hbm, saved), (cotangent_hbm, cotangent),
            (gains_hbm, gains), (entering_hbm, entering), (cot_entering_hbm, cot_entering),
        ))
    ]
    for copy in small:
        copy.start()
    loads = [
        pltpu.make_async_copy(
            source.at[0, 0, :, pl.ds(h * width, width)], target.at[h], load_sem.at[2 * n + h]
        )
        for n, (source, target) in enumerate(((up_rows, up), (down_rows, down)))
        for h in range(2)
    ]
    for load in loads:
        load.start()

    def send(source, target, send_sem, recv_sem, device_id):
        pltpu.make_async_remote_copy(
            src_ref=source, dst_ref=target, send_sem=send_sem, recv_sem=recv_sem,
            device_id=device_id, device_id_type=MESH,
        ).start()

    def arrived(like, recv_sem):
        pltpu.make_async_remote_copy(
            src_ref=like, dst_ref=like, send_sem=recv_sem, recv_sem=recv_sem,
            device_id=mirror, device_id_type=MESH,
        ).wait_recv()

    def departed(like, send_sem):
        pltpu.make_async_remote_copy(
            src_ref=like, dst_ref=like, send_sem=send_sem, recv_sem=send_sem,
            device_id=mirror, device_id_type=MESH,
        ).wait_send()

    blocks = {2: from_prev.at[0, 0, 0:2], 4: from_prev.at[0, 0], 6: scattered.at[0], 8: from_prev.at[0], 16: from_prev.at[0:2], 24: from_prev.at[0:3]}

    inner, outer = ("x", "z"), ("z", "x")
    low, high, whole = pl.ds(0, half), pl.ds(half, half), pl.ds(0, width)

    def slab(ref, index, h, step, lanes):
        at = (place[outer[h]] + step) % RING
        return ref.at[index, h, at, :, :, lanes] if h == 0 else ref.at[index, h, :, at, :, lanes]

    def block(ref, index, h, step):
        at = dict(place)
        at[inner[h]] = (place[inner[h]] + step) % RING
        return ref.at[index, h, at["z"], at["x"]]

    def gather_inner(a):
        for step in (1, 3) if a in PASSED else (1, 3, 2):
            for h in range(2):
                own = block(gathered, a, h, 0)
                send(own, own, ag_send.at[a, 0], ag_recv.at[a, 0], along(inner[h], step))

    def gather_pass(a):
        arrived(blocks[4], ag_recv.at[a, 0])
        for h in range(2):
            for step, lanes in ((1, low), (-1, high)):
                passed = block(gathered, a, h, -step).at[:, lanes]
                send(passed, passed, ag_send.at[a, 0], ag_recv.at[a, 3], along(inner[h], step))

    def gather_outer(a):
        if a in PASSED:
            arrived(blocks[2], ag_recv.at[a, 3])
        else:
            arrived(blocks[6], ag_recv.at[a, 0])
        for n, group in ((1, ((1, low), (-1, high))), (2, ((1, high), (-1, low)))):
            for h in range(2):
                for step, lanes in group:
                    own = slab(gathered, a, h, 0, lanes)
                    send(own, own, ag_send.at[a, 1], ag_recv.at[a, n], along(outer[h], step))

    def gather_relay(a):
        arrived(blocks[8], ag_recv.at[a, 1])
        for h in range(2):
            for step, lanes in ((1, low), (-1, high)):
                passed = slab(gathered, a, h, -step, lanes)
                send(passed, passed, ag_send.at[a, 1], ag_recv.at[a, 2], along(outer[h], step))

    def gather_end(a):
        arrived(blocks[16], ag_recv.at[a, 2])

    def scatter_start(p, h):
        for n, step, lanes, target, to in (
            (0, 2, low, pass_on, 1),
            (0, 2, high, pass_on, -1),
            (1, 1, high, from_prev, 1),
            (1, -1, low, from_next, -1),
        ):
            send(
                slab(partial, p, h, step, lanes), target.at[p, h, :, :, lanes],
                rs_send.at[p, 1], rs_recv.at[p, n], along(outer[h], to),
            )

    def scatter_relay(p):
        arrived(blocks[8], rs_recv.at[p, 0])
        for h in range(2):
            for step, lanes, target in ((1, low, from_prev), (-1, high, from_next)):
                mine = slab(partial, p, h, step, lanes)
                passing = pass_on[p, h, :, :, lanes].astype(F32)
                mine[...] = (mine[...].astype(F32) + passing).astype(BF16)
                send(
                    mine, target.at[p, h, :, :, lanes],
                    rs_send.at[p, 1], rs_recv.at[p, 1], along(outer[h], step),
                )

    def scatter_out(p):
        arrived(blocks[16], rs_recv.at[p, 1])
        for h in range(2):
            total = slab(partial, p, h, 0, whole)[...].astype(F32)
            total = total + from_prev[p, h].astype(F32) + from_next[p, h].astype(F32)
            total = total.reshape(RING, 2, 8, width)
            for direction in range(2):
                part = total[:, direction]
                part = jnp.concatenate([part[:, :, :half], part[:, :, half:]], axis=1)
                split_out[p % 2, h, direction] = part.astype(BF16)
            for step in (1, 3, 2, 0):
                at = (place[inner[h]] + step) % RING
                sems = (rs_send.at[p, 0], rs_recv.at[p, 2])
                for direction in range(2):
                    if direction or step:
                        to = far_along(inner[h], step) if direction else along(inner[h], step)
                        slot = 3 + step if direction else step - 1
                        send(split_out.at[p % 2, h, direction, at], split_in.at[p % 2, h, slot], *sems, to)

    def scatter_in(p):
        arrived(split_in.at[0], rs_recv.at[p, 2])
        sums = []
        for direction in range(2):
            halves = []
            for h in range(2):
                parts = [split_in[p % 2, h, slot] for slot in (range(3, 7) if direction else range(3))]
                if not direction:
                    parts.append(split_out[p % 2, h, 0, pl.ds(place[inner[h]], 1)][0])
                total = sum(part.astype(F32) for part in parts)
                halves += [total[:8], total[8:]]
            sums.append(jnp.concatenate(halves, axis=1))
        return sums

    def scatter_inner(p):
        if p >= 2:
            return scatter_out(p)
        arrived(blocks[16], rs_recv.at[p, 1])
        for h in range(2):
            total = slab(partial, p, h, 0, whole)[...].astype(F32)
            total = total + from_prev[p, h].astype(F32) + from_next[p, h].astype(F32)
            summed[p, h] = total.astype(BF16)
            for step in (1, 3, 2):
                at = (place[inner[h]] + step) % RING
                send(
                    summed.at[p, h, at], scattered.at[p, h, step - 1],
                    rs_send.at[p, 0], rs_recv.at[p, 2], along(inner[h], step),
                )

    def scatter_end(p):
        arrived(blocks[6], rs_recv.at[p, 2])
        halves = []
        for h in range(2):
            total = summed[p, h, pl.ds(place[inner[h]], 1)][0].astype(F32)
            for step in (1, 2, 3):
                total = total + scattered[p, h, step - 1].astype(F32)
            halves.append(total)
        return jnp.concatenate(halves, axis=1)

    def put_block(a, value):
        value = value.astype(BF16)
        for h in range(2):
            block(gathered, a, h, 0)[...] = value[:, h * width : (h + 1) * width]

    def factor_of(value):
        return lax.rsqrt(mean(value * value) + EPSILON)

    def normed(value):
        return value * factor_of(value) * gain

    def norm_back(own, upstream, scaling, d_normed):
        scaled = d_normed * scaling
        factor = factor_of(own)
        unit = own * factor
        return upstream + factor * (scaled - unit * mean(unit * scaled))

    def tokens(a, h):
        return gathered[a, h].reshape(RING * RING * 16, width)

    def onto_units(a, weights):
        return contract_last(tokens(a, 0), weights[0]) + contract_last(tokens(a, 1), weights[1])

    def onto_features(p, h, value, weights):
        tile = 256
        for n in range(width // tile):
            lanes = pl.ds(n * tile, tile)
            product = jnp.dot(value, weights[h, :, lanes], preferred_element_type=F32)
            partial[p, h, :, :, :, lanes] = product.astype(BF16).reshape(RING, RING, 16, tile)
        scatter_start(p, h)

    loaded = set()

    def weights_of(n):
        if n not in loaded:
            loaded.add(n)
            for load in loads[2 * n : 2 * n + 2]:
                load.wait()
        return (up, down)[n]

    def pairs(value):
        return value.reshape(RING * RING, 2, 8, units)

    def hidden_near(direction):
        gather_end(direction)
        hidden = pairs(onto_units(direction, weights_of(0)))
        for n in range(2):
            near[n, :, direction] = hidden[:, n]

    def hidden_forward(period):
        if period == 0:
            hidden = near[0].reshape(-1, units)
        else:
            gather_end(FB)
            hidden = onto_units(FB, weights_of(0))
        active[...] = (hidden * jax.nn.sigmoid(hidden)).astype(BF16)

    def hidden_backward(period):
        if period == 0:
            hidden = near[1].reshape(-1, units)
        else:
            gather_end(NB)
            hidden = onto_units(NB, weights_of(0))
        gating = jax.nn.sigmoid(hidden)
        flipped[3 + period] = (hidden * gating).astype(BF16).T
        bent[period] = gating * (1.0 + hidden * (1.0 - gating))

    def slope(period):
        gather_end(GS[period])
        slopes[period] = (onto_units(GS[period], weights_of(1)) * bent[period]).astype(BF16)

    def keep_slope(period):
        if period == 1:
            flipped[2] = slopes[1].T
            return
        value = pairs(wide(slopes[0]))
        for direction in range(2):
            mine = value[:, direction]
            mine = jnp.stack([jnp.zeros_like(mine), mine], axis=1).reshape(-1, units)
            flipped[direction] = mine.astype(BF16).T

    def weight_grad(first, arrays, h, target):
        tile = 256
        left = jnp.concatenate([flipped[first + n] for n in range(len(arrays))], axis=1)
        for n in range(width // tile):
            lanes = pl.ds(n * tile, tile)
            right = jnp.concatenate(
                [gathered[a, h, :, :, :, lanes].reshape(-1, tile) for a in arrays], axis=0
            )
            total = jnp.dot(left, right, preferred_element_type=F32)
            target[0, :, pl.ds(h * width + n * tile, tile)] = total.astype(BF16)

    def wide(value):
        return value.astype(F32)

    def folded(value):
        return jnp.concatenate([wide(value)[:, :width], wide(value)[:, width:]], axis=0).astype(BF16)

    def unfolded(value):
        return jnp.concatenate([wide(value)[:8], wide(value)[8:]], axis=1)

    def far_ready(n):
        send(far_out.at[n], far_in.at[n], far_send.at[0], far_recv.at[n], mirror)

    def far_send_one(n, value):
        far_out[n] = folded(value)
        far_ready(n)

    def from_far(n):
        arrived(far_in.at[n], far_recv.at[n])
        return unfolded(far_in[n])

    def with_far(own, n):
        return jnp.concatenate([wide(own), from_far(n)], axis=0)

    def hop(n, value, to):
        hop_out[n] = value

        @pl.when(s != (0 if n else sections - 1))
        def _():
            send(hop_out.at[n], hop_in.at[n], hop_send.at[n], hop_recv.at[n], to)

    def hopped(n, entered, edge):
        @pl.when(s == edge)
        def _():
            landed[...] = joined(entered[0])

        @pl.when(s != edge)
        def _():
            arrived(hop_in.at[n], hop_recv.at[n])
            landed[...] = wide(hop_in[n])

        return landed[...]

    def deliver(n, target, period, value):
        mirror_out[n] = folded(value[8:])
        send(mirror_out.at[n], mirror_in.at[n], mirror_send.at[0], mirror_recv.at[n], mirror)
        target[period, 0, 0] = value[:8].astype(BF16)

    def delivered(n, target, period):
        arrived(mirror_in.at[n], mirror_recv.at[n])
        target[period, 1, 0] = unfolded(mirror_in[n]).astype(BF16)

    def rounded(value):
        return wide(value.astype(BF16))

    def finish_forward(period):
        if period == 1:
            near_sum, far_sum = scatter_in(2)
            states_out[1, 0, 0] = (rows[FB, 0:8] + near_sum).astype(BF16)
            states_out[1, 1, 0] = (from_far(4) + far_sum).astype(BF16)
            return
        produced = rounded(rows[NEAR_FORWARD] + scatter_end(0))
        hop(0, produced.astype(BF16), after)
        deliver(0, states_out, 0, produced)

    def finish_backward(period):
        if period == 1:
            near_sum, far_sum = scatter_in(3)
            back = norm_back(rows[NB, 0:8], rows[GB, 0:8], gain, near_sum)
            input_grads[1, 0, 0] = back.astype(BF16)
            back = norm_back(wide(saved[1, 1, 0]), from_far(5), far_gain, far_sum)
            input_grads[1, 1, 0] = back.astype(BF16)
            return
        back = rounded(norm_back(rows[NEAR_SAVED], rows[GA], gain, scatter_end(1)))
        hop(1, back.astype(BF16), before)
        deliver(1, input_grads, 0, back)

    def begin(a, value):
        rows[a] = value
        put_block(a, value if a in GS else normed(value))
        gather_inner(a)

    def begin_near(direction, forward, kept):
        own = pl.ds(8 * direction, 8)
        rows[NEAR_FORWARD, own] = forward
        rows[NEAR_SAVED, own] = kept
        put_block(direction, normed(jnp.concatenate([forward, kept], axis=0)))

    def joined(pair):
        return jnp.concatenate([wide(pair[0]), wide(pair[1])], axis=0)

    def begin_later_forward():
        begin(FB, hopped(0, entering, 0))
        far_send_one(4, rows[FB, 8:16])

    def begin_later_grads():
        begin(GB, hopped(1, cot_entering, sections - 1))
        far_send_one(5, rows[GB, 8:16])

    def begin_far():
        begin_near(D1, from_far(0), from_far(1))
        gather_inner(D1)

    def far_rest():
        far_ready(2)
        far_ready(3)

    def end():
        delivered(0, states_out, 0)
        delivered(1, input_grads, 0)
        for like, sem in ((far_out, far_send), (mirror_out, mirror_send)):
            departed(like, sem.at[0])

        @pl.when(s != sections - 1)
        def _():
            departed(hop_out.at[0], hop_send.at[0])

        @pl.when(s != 0)
        def _():
            departed(hop_out.at[1], hop_send.at[1])

        for sem, count in ((ag_send, 6), (rs_send, 4)):
            for n in range(count):
                departed(split_in.at[0] if sem is rs_send and n >= 2 else blocks[6], sem.at[n, 0])
                departed(blocks[24], sem.at[n, 1])

    def gain_of(layer):
        chosen = lax.broadcasted_iota(jnp.int32, gains.shape, 0) == layer
        return jnp.sum(jnp.where(chosen, wide(gains[...]), 0.0), axis=0, keepdims=True)

    for copy in small:
        copy.wait()
    gain, far_gain = gain_of(s), gain_of(far)
    steps = {
        "far0": lambda: far_ready(0),
        "far1": lambda: far_ready(1),
        "far2": far_rest,
        "nD0": lambda: gather_inner(D0),
        "nD1": begin_far,
        "nG0": lambda: begin(GA, with_far(cotangent[0, 0], 2)),
        "nN1": lambda: begin(NB, with_far(saved[1, 0, 0], 3)),
        "hD0": lambda: hidden_near(D0),
        "hD1": lambda: hidden_near(D1),
        "nF1": begin_later_forward,
        "nG1": begin_later_grads,
        "w1a": lambda: weight_grad(3, (GA, GB), 0, grad_down),
        "w1b": lambda: weight_grad(3, (GA, GB), 1, grad_down),
        "w0a": lambda: weight_grad(0, (D0, D1, NB), 0, grad_up),
        "w0b": lambda: weight_grad(0, (D0, D1, NB), 1, grad_up),
        "end": end,
    }
    for a, name in enumerate(("D0", "D1", "G0", "N1", "F1", "G1")):
        steps["ir" + name] = functools.partial(gather_pass, a)
        steps["out" + name] = functools.partial(gather_outer, a)
        steps["rel" + name] = functools.partial(gather_relay, a)
    for period in range(2):
        k = str(period)
        steps["hF" + k] = functools.partial(hidden_forward, period)
        steps["hB" + k] = functools.partial(hidden_backward, period)
        steps["gB" + k] = functools.partial(slope, period)
        steps["keepB" + k] = functools.partial(keep_slope, period)
        steps["finF" + k] = functools.partial(finish_forward, period)
        steps["finB" + k] = functools.partial(finish_backward, period)
        for h in range(2):
            steps[f"pF{k}h{h}"] = lambda p=2 * period, h=h: onto_features(p, h, active[...], weights_of(1))
            steps[f"pB{k}h{h}"] = lambda p=2 * period + 1, h=h: onto_features(
                p, h, slopes[p // 2], weights_of(0)
            )
        for n, name in enumerate("FB"):
            steps["rsr" + name + k] = functools.partial(scatter_relay, 2 * period + n)
            steps["rsi" + name + k] = functools.partial(scatter_inner, 2 * period + n)
    for n, value in enumerate((states_in[1, 0], saved[0, 1, 0], cotangent[1, 0], saved[1, 1, 0])):
        far_out[n] = folded(value)
    begin_near(D0, wide(states_in[0, 0]), wide(saved[0, 0, 0]))
    pl.semaphore_wait(barrier, len(partners))
    for name in ORDER:
        steps[name]()


def write_out(*refs):
    sems = refs[-1]
    copies = [pltpu.make_async_copy(refs[n], refs[4 + n], sems.at[n]) for n in range(4)]
    for copy in copies:
        copy.start()
    for copy in copies:
        copy.wait()


def body(states_in, entering, saved, cotangent, cot_entering, gains, up_rows, down_rows):
    units, features = up_rows.shape[2:]
    width = features // 2
    dma, vmem = pltpu.SemaphoreType.DMA, pltpu.VMEM
    in_vmem = pl.BlockSpec(memory_space=pltpu.VMEM)
    anywhere = pl.BlockSpec(memory_space=pl.ANY)
    grid_rows = (RING, RING, 16, width)
    shapes = (saved.shape, saved.shape, (1, units, features), (1, units, features))
    results = pl.pallas_call(
        kernel,
        out_shape=tuple(vmem(shape, BF16) for shape in shapes),
        in_specs=[anywhere] * 8,
        out_specs=(in_vmem,) * 4,
        scratch_shapes=[
            vmem((2, units, width), BF16),
            vmem((2, units, width), BF16),
            vmem((6, 2) + grid_rows, BF16),
            vmem((4, 2) + grid_rows, BF16),
            vmem((4, 2) + grid_rows[1:], BF16),
            vmem((4, 2) + grid_rows[1:], BF16),
            vmem((4, 2) + grid_rows[1:], BF16),
            vmem((4, 2) + grid_rows[1:], BF16),
            vmem((4, 2, 3, 16, width), BF16),
            vmem((2, 2, 2, RING, 16, width // 2), BF16),
            vmem((2, 2, 7, 16, width // 2), BF16),
            vmem((6, 16, features), F32),
            vmem((6, 16, width), BF16),
            vmem((6, 16, width), BF16),
            vmem((2, 16, features), BF16),
            vmem((2, 16, features), BF16),
            vmem((16, features), F32),
            vmem((2, 16, width), BF16),
            vmem((2, 16, width), BF16),
            vmem((2, 256, units), BF16),
            vmem((2, 256, units), F32),
            vmem((256, units), BF16),
            vmem((5, units, 256), BF16),
            vmem((2, 16, 2, 8, units), F32),
            vmem(states_in.shape, BF16),
            vmem(entering.shape, BF16),
            vmem(saved.shape, BF16),
            vmem(cotangent.shape, BF16),
            vmem(cot_entering.shape, BF16),
            vmem(gains.shape, BF16),
            dma((4,)),
            dma((6,)),
            dma((6, 2)),
            dma((6, 4)),
            dma((4, 2)),
            dma((4, 3)),
            dma((1,)),
            dma((6,)),
            dma((2,)),
            dma((2,)),
            dma((1,)),
            dma((2,)),
        ],
        compiler_params=pltpu.CompilerParams(
            collective_id=0, has_side_effects=True, vmem_limit_bytes=48 * 2**20
        ),
        cost_estimate=pl.CostEstimate(flops=15 * 10**9, bytes_accessed=17 * 10**6, transcendentals=0),
    )(states_in, entering, saved, cotangent, cot_entering, gains, up_rows, down_rows)
    return pl.pallas_call(
        write_out,
        out_shape=tuple(jax.ShapeDtypeStruct(shape, BF16) for shape in shapes),
        in_specs=[in_vmem] * 4,
        out_specs=(anywhere,) * 4,
        scratch_shapes=[dma((4,))],
        compiler_params=pltpu.CompilerParams(vmem_limit_bytes=4 * 2**20),
    )(*results)


def solution(mesh):
    group = ("dp", "tensor")
    placed = (
        P(None, "section", group, None),
        P(None, None, group, None),
        P(None, None, "section", group, None),
        P(None, "section", group, None),
        P(None, None, group, None),
        P(),
        P("section", None, group, None),
        P("section", None, group, None),
    )
    return jax.shard_map(
        body,
        mesh=mesh,
        in_specs=placed,
        out_specs=(
            P(None, None, "section", group, None),
            P(None, None, "section", group, None),
            P("section", group, None),
            P("section", group, None),
        ),
        check_vma=False,
    )
```

```python
import functools

import jax
import jax.numpy as jnp
from jax import lax
from jax.experimental import pallas as pl
from jax.experimental.pallas import tpu as pltpu
from jax.sharding import PartitionSpec as P

EPSILON = 1e-06
MESH = pl.DeviceIdType.MESH
F32, BF16 = jnp.float32, jnp.bfloat16
D0, D1, GA, NB, FB, GB = range(6)
NEAR_FORWARD, NEAR_SAVED = 0, 1
FS, NS, GS = (NEAR_FORWARD, FB), (NEAR_SAVED, NB), (GA, GB)
PASSED = (GA, NB, D1, GB,)
RING = 4

ORDER = (
    "far0", "far1", "nD0", "nD1", "outD0", "far2", "irD1", "nG0", "relD0", "outD1", "hD0", "irG0",
    "relD1", "outG0", "hD1", "hF0", "relG0", "pF0h0", "pF0h1", "nN1", "hB0", "gB0", "rsrF0",
    "pB0h0", "pB0h1", "rsrB0", "rsiF0", "irN1", "rsiB0", "finF0", "outN1", "keepB0", "finB0",
    "nF1", "relN1", "nG1", "outF1", "irG1", "hB1", "relF1", "outG1", "hF1", "relG1", "pF1h0",
    "pF1h1", "gB1", "pB1h0", "pB1h1", "keepB1", "rsrF1", "w0a", "w1a", "rsrB1", "w1b", "rsiF1",
    "rsiB1", "w0b", "finF1", "finB1", "end",
)


def contract_last(former, latter):
    return lax.dot_general(former, latter, (((1,), (1,)), ((), ())), preferred_element_type=F32)


def mean(value):
    return jnp.mean(value, axis=-1, keepdims=True)


def kernel(
    states_in_hbm, entering_hbm, saved_hbm, cotangent_hbm, cot_entering_hbm, gains_hbm, up_rows, down_rows,
    states_out, input_grads, grad_up, grad_down,
    up, down, gathered, partial, pass_on, from_prev, from_next, summed, scattered,
    split_out, split_in, rows, far_out, far_in, hop_out, hop_in, landed, mirror_out, mirror_in,
    slopes, bent, active, flipped, near,
    states_in, entering, saved, cotangent, cot_entering, gains, load_sem, small_sem, ag_send, ag_recv, rs_send, rs_recv, far_send, far_recv,
    hop_send, hop_recv, mirror_send, mirror_recv,
):
    s = lax.axis_index("section")
    d = lax.axis_index("dp")
    t = lax.axis_index("tensor")
    sections = lax.axis_size("section")
    width = up.shape[-1]
    half = width // 2
    features = 2 * width
    units = up.shape[1]
    place = {"x": d % RING, "z": (d // RING) * 2 + t}

    far = sections - 1 - s

    def device(section, x, z):
        return (section, (z // 2) * RING + x, z % 2)

    def moved(section, axis, step):
        to = dict(place)
        to[axis] = (place[axis] + step) % RING
        return device(section, to["x"], to["z"])

    steps_away = [(axis, step) for axis in "xz" for step in (1, 2, 3)]
    neighbours = {away: moved(s, *away) for away in steps_away}
    far_neighbours = {away: moved(far, *away) for away in steps_away}
    mirror = device(far, place["x"], place["z"])

    def along(axis, step):
        return neighbours[axis, step % RING]

    def far_along(axis, step):
        return far_neighbours[axis, step] if step else mirror

    after = device((s + 1) % sections, place["x"], place["z"])
    before = device((s + sections - 1) % sections, place["x"], place["z"])

    barrier = pltpu.get_barrier_semaphore()
    partners = list(neighbours.values()) + list(far_neighbours.values()) + [mirror, after, before]
    for partner in partners:
        pl.semaphore_signal(barrier, inc=1, device_id=partner, device_id_type=MESH)
    small = [
        pltpu.make_async_copy(source, target, small_sem.at[n])
        for n, (source, target) in enumerate((
            (states_in_hbm, states_in), (saved_hbm, saved), (cotangent_hbm, cotangent),
            (gains_hbm, gains), (entering_hbm, entering), (cot_entering_hbm, cot_entering),
        ))
    ]
    for copy in small:
        copy.start()
    loads = [
        pltpu.make_async_copy(
            source.at[0, 0, :, pl.ds(h * width, width)], target.at[h], load_sem.at[2 * n + h]
        )
        for n, (source, target) in enumerate(((up_rows, up), (down_rows, down)))
        for h in range(2)
    ]
    for load in loads:
        load.start()

    def send(source, target, send_sem, recv_sem, device_id):
        pltpu.make_async_remote_copy(
            src_ref=source, dst_ref=target, send_sem=send_sem, recv_sem=recv_sem,
            device_id=device_id, device_id_type=MESH,
        ).start()

    def arrived(like, recv_sem):
        pltpu.make_async_remote_copy(
            src_ref=like, dst_ref=like, send_sem=recv_sem, recv_sem=recv_sem,
            device_id=mirror, device_id_type=MESH,
        ).wait_recv()

    def departed(like, send_sem):
        pltpu.make_async_remote_copy(
            src_ref=like, dst_ref=like, send_sem=send_sem, recv_sem=send_sem,
            device_id=mirror, device_id_type=MESH,
        ).wait_send()

    blocks = {2: from_prev.at[0, 0, 0:2], 4: from_prev.at[0, 0], 6: scattered.at[0], 8: from_prev.at[0], 16: from_prev.at[0:2], 24: from_prev.at[0:3]}

    inner, outer = ("x", "z"), ("z", "x")
    low, high, whole = pl.ds(0, half), pl.ds(half, half), pl.ds(0, width)

    def slab(ref, index, h, step, lanes):
        at = (place[outer[h]] + step) % RING
        return ref.at[index, h, at, :, :, lanes] if h == 0 else ref.at[index, h, :, at, :, lanes]

    def block(ref, index, h, step):
        at = dict(place)
        at[inner[h]] = (place[inner[h]] + step) % RING
        return ref.at[index, h, at["z"], at["x"]]

    def gather_inner(a):
        for step in (1, 3) if a in PASSED else (1, 3, 2):
            for h in range(2):
                own = block(gathered, a, h, 0)
                send(own, own, ag_send.at[a, 0], ag_recv.at[a, 0], along(inner[h], step))

    def gather_pass(a):
        arrived(blocks[4], ag_recv.at[a, 0])
        for h in range(2):
            for step, lanes in ((1, low), (-1, high)):
                passed = block(gathered, a, h, -step).at[:, lanes]
                send(passed, passed, ag_send.at[a, 0], ag_recv.at[a, 3], along(inner[h], step))

    def gather_outer(a):
        if a in PASSED:
            arrived(blocks[2], ag_recv.at[a, 3])
        else:
            arrived(blocks[6], ag_recv.at[a, 0])
        for n, group in ((1, ((1, low), (-1, high))), (2, ((1, high), (-1, low)))):
            for h in range(2):
                for step, lanes in group:
                    own = slab(gathered, a, h, 0, lanes)
                    send(own, own, ag_send.at[a, 1], ag_recv.at[a, n], along(outer[h], step))

    def gather_relay(a):
        arrived(blocks[8], ag_recv.at[a, 1])
        for h in range(2):
            for step, lanes in ((1, low), (-1, high)):
                passed = slab(gathered, a, h, -step, lanes)
                send(passed, passed, ag_send.at[a, 1], ag_recv.at[a, 2], along(outer[h], step))

    def gather_end(a):
        arrived(blocks[16], ag_recv.at[a, 2])

    def scatter_start(p, h):
        for n, step, lanes, target, to in (
            (0, 2, low, pass_on, 1),
            (0, 2, high, pass_on, -1),
            (1, 1, high, from_prev, 1),
            (1, -1, low, from_next, -1),
        ):
            send(
                slab(partial, p, h, step, lanes), target.at[p, h, :, :, lanes],
                rs_send.at[p, 1], rs_recv.at[p, n], along(outer[h], to),
            )

    def scatter_relay(p):
        arrived(blocks[8], rs_recv.at[p, 0])
        for h in range(2):
            for step, lanes, target in ((1, low, from_prev), (-1, high, from_next)):
                mine = slab(partial, p, h, step, lanes)
                passing = pass_on[p, h, :, :, lanes].astype(F32)
                mine[...] = (mine[...].astype(F32) + passing).astype(BF16)
                send(
                    mine, target.at[p, h, :, :, lanes],
                    rs_send.at[p, 1], rs_recv.at[p, 1], along(outer[h], step),
                )

    def scatter_out(p):
        arrived(blocks[16], rs_recv.at[p, 1])
        for h in range(2):
            total = slab(partial, p, h, 0, whole)[...].astype(F32)
            total = total + from_prev[p, h].astype(F32) + from_next[p, h].astype(F32)
            total = total.reshape(RING, 2, 8, width)
            for direction in range(2):
                part = total[:, direction]
                part = jnp.concatenate([part[:, :, :half], part[:, :, half:]], axis=1)
                split_out[p % 2, h, direction] = part.astype(BF16)
            for step in (1, 3, 2, 0):
                at = (place[inner[h]] + step) % RING
                sems = (rs_send.at[p, 0], rs_recv.at[p, 2])
                for direction in range(2):
                    if direction or step:
                        to = far_along(inner[h], step) if direction else along(inner[h], step)
                        slot = 3 + step if direction else step - 1
                        send(split_out.at[p % 2, h, direction, at], split_in.at[p % 2, h, slot], *sems, to)

    def scatter_in(p):
        arrived(split_in.at[0], rs_recv.at[p, 2])
        sums = []
        for direction in range(2):
            halves = []
            for h in range(2):
                parts = [split_in[p % 2, h, slot] for slot in (range(3, 7) if direction else range(3))]
                if not direction:
                    parts.append(split_out[p % 2, h, 0, pl.ds(place[inner[h]], 1)][0])
                total = sum(part.astype(F32) for part in parts)
                halves += [total[:8], total[8:]]
            sums.append(jnp.concatenate(halves, axis=1))
        return sums

    def scatter_inner(p):
        if p >= 2:
            return scatter_out(p)
        arrived(blocks[16], rs_recv.at[p, 1])
        for h in range(2):
            total = slab(partial, p, h, 0, whole)[...].astype(F32)
            total = total + from_prev[p, h].astype(F32) + from_next[p, h].astype(F32)
            summed[p, h] = total.astype(BF16)
            for step in (1, 3, 2):
                at = (place[inner[h]] + step) % RING
                send(
                    summed.at[p, h, at], scattered.at[p, h, step - 1],
                    rs_send.at[p, 0], rs_recv.at[p, 2], along(inner[h], step),
                )

    def scatter_end(p):
        arrived(blocks[6], rs_recv.at[p, 2])
        halves = []
        for h in range(2):
            total = summed[p, h, pl.ds(place[inner[h]], 1)][0].astype(F32)
            for step in (1, 2, 3):
                total = total + scattered[p, h, step - 1].astype(F32)
            halves.append(total)
        return jnp.concatenate(halves, axis=1)

    def put_block(a, value):
        value = value.astype(BF16)
        for h in range(2):
            block(gathered, a, h, 0)[...] = value[:, h * width : (h + 1) * width]

    def factor_of(value):
        return lax.rsqrt(mean(value * value) + EPSILON)

    def normed(value):
        return value * factor_of(value) * gain

    def norm_back(own, upstream, scaling, d_normed):
        scaled = d_normed * scaling
        factor = factor_of(own)
        unit = own * factor
        return upstream + factor * (scaled - unit * mean(unit * scaled))

    def tokens(a, h):
        return gathered[a, h].reshape(RING * RING * 16, width)

    def onto_units(a, weights):
        return contract_last(tokens(a, 0), weights[0]) + contract_last(tokens(a, 1), weights[1])

    def onto_features(p, h, value, weights):
        tile = 256
        for n in range(width // tile):
            lanes = pl.ds(n * tile, tile)
            product = jnp.dot(value, weights[h, :, lanes], preferred_element_type=F32)
            partial[p, h, :, :, :, lanes] = product.astype(BF16).reshape(RING, RING, 16, tile)
        scatter_start(p, h)

    loaded = set()

    def weights_of(n):
        if n not in loaded:
            loaded.add(n)
            for load in loads[2 * n : 2 * n + 2]:
                load.wait()
        return (up, down)[n]

    def pairs(value):
        return value.reshape(RING * RING, 2, 8, units)

    def hidden_near(direction):
        gather_end(direction)
        hidden = pairs(onto_units(direction, weights_of(0)))
        for n in range(2):
            near[n, :, direction] = hidden[:, n]

    def hidden_forward(period):
        if period == 0:
            hidden = near[0].reshape(-1, units)
        else:
            gather_end(FB)
            hidden = onto_units(FB, weights_of(0))
        active[...] = (hidden * jax.nn.sigmoid(hidden)).astype(BF16)

    def hidden_backward(period):
        if period == 0:
            hidden = near[1].reshape(-1, units)
        else:
            gather_end(NB)
            hidden = onto_units(NB, weights_of(0))
        gating = jax.nn.sigmoid(hidden)
        flipped[3 + period] = (hidden * gating).astype(BF16).T
        bent[period] = gating * (1.0 + hidden * (1.0 - gating))

    def slope(period):
        gather_end(GS[period])
        slopes[period] = (onto_units(GS[period], weights_of(1)) * bent[period]).astype(BF16)

    def keep_slope(period):
        if period == 1:
            flipped[2] = slopes[1].T
            return
        value = pairs(wide(slopes[0]))
        for direction in range(2):
            mine = value[:, direction]
            mine = jnp.stack([jnp.zeros_like(mine), mine], axis=1).reshape(-1, units)
            flipped[direction] = mine.astype(BF16).T

    def weight_grad(first, arrays, h, target):
        tile = 256
        left = jnp.concatenate([flipped[first + n] for n in range(len(arrays))], axis=1)
        for n in range(width // tile):
            lanes = pl.ds(n * tile, tile)
            right = jnp.concatenate(
                [gathered[a, h, :, :, :, lanes].reshape(-1, tile) for a in arrays], axis=0
            )
            total = jnp.dot(left, right, preferred_element_type=F32)
            target[0, :, pl.ds(h * width + n * tile, tile)] = total.astype(BF16)

    def wide(value):
        return value.astype(F32)

    def folded(value):
        return jnp.concatenate([wide(value)[:, :width], wide(value)[:, width:]], axis=0).astype(BF16)

    def unfolded(value):
        return jnp.concatenate([wide(value)[:8], wide(value)[8:]], axis=1)

    def far_ready(n):
        send(far_out.at[n], far_in.at[n], far_send.at[0], far_recv.at[n], mirror)

    def far_send_one(n, value):
        far_out[n] = folded(value)
        far_ready(n)

    def from_far(n):
        arrived(far_in.at[n], far_recv.at[n])
        return unfolded(far_in[n])

    def with_far(own, n):
        return jnp.concatenate([wide(own), from_far(n)], axis=0)

    def hop(n, value, to):
        hop_out[n] = value

        @pl.when(s != (0 if n else sections - 1))
        def _():
            send(hop_out.at[n], hop_in.at[n], hop_send.at[n], hop_recv.at[n], to)

    def hopped(n, entered, edge):
        @pl.when(s == edge)
        def _():
            landed[...] = joined(entered[0])

        @pl.when(s != edge)
        def _():
            arrived(hop_in.at[n], hop_recv.at[n])
            landed[...] = wide(hop_in[n])

        return landed[...]

    def deliver(n, target, period, value):
        mirror_out[n] = folded(value[8:])
        send(mirror_out.at[n], mirror_in.at[n], mirror_send.at[0], mirror_recv.at[n], mirror)
        target[period, 0, 0] = value[:8].astype(BF16)

    def delivered(n, target, period):
        arrived(mirror_in.at[n], mirror_recv.at[n])
        target[period, 1, 0] = unfolded(mirror_in[n]).astype(BF16)

    def rounded(value):
        return wide(value.astype(BF16))

    def finish_forward(period):
        if period == 1:
            near_sum, far_sum = scatter_in(2)
            states_out[1, 0, 0] = (rows[FB, 0:8] + near_sum).astype(BF16)
            states_out[1, 1, 0] = (from_far(4) + far_sum).astype(BF16)
            return
        produced = rounded(rows[NEAR_FORWARD] + scatter_end(0))
        hop(0, produced.astype(BF16), after)
        deliver(0, states_out, 0, produced)

    def finish_backward(period):
        if period == 1:
            near_sum, far_sum = scatter_in(3)
            back = norm_back(rows[NB, 0:8], rows[GB, 0:8], gain, near_sum)
            input_grads[1, 0, 0] = back.astype(BF16)
            back = norm_back(wide(saved[1, 1, 0]), from_far(5), far_gain, far_sum)
            input_grads[1, 1, 0] = back.astype(BF16)
            return
        back = rounded(norm_back(rows[NEAR_SAVED], rows[GA], gain, scatter_end(1)))
        hop(1, back.astype(BF16), before)
        deliver(1, input_grads, 0, back)

    def begin(a, value):
        rows[a] = value
        put_block(a, value if a in GS else normed(value))
        gather_inner(a)

    def begin_near(direction, forward, kept):
        own = pl.ds(8 * direction, 8)
        rows[NEAR_FORWARD, own] = forward
        rows[NEAR_SAVED, own] = kept
        put_block(direction, normed(jnp.concatenate([forward, kept], axis=0)))

    def joined(pair):
        return jnp.concatenate([wide(pair[0]), wide(pair[1])], axis=0)

    def begin_later_forward():
        begin(FB, hopped(0, entering, 0))
        far_send_one(4, rows[FB, 8:16])

    def begin_later_grads():
        begin(GB, hopped(1, cot_entering, sections - 1))
        far_send_one(5, rows[GB, 8:16])

    def begin_far():
        begin_near(D1, from_far(0), from_far(1))
        gather_inner(D1)

    def far_rest():
        far_ready(2)
        far_ready(3)

    def end():
        delivered(0, states_out, 0)
        delivered(1, input_grads, 0)
        for like, sem in ((far_out, far_send), (mirror_out, mirror_send)):
            departed(like, sem.at[0])

        @pl.when(s != sections - 1)
        def _():
            departed(hop_out.at[0], hop_send.at[0])

        @pl.when(s != 0)
        def _():
            departed(hop_out.at[1], hop_send.at[1])

        for sem, count in ((ag_send, 6), (rs_send, 4)):
            for n in range(count):
                departed(split_in.at[0] if sem is rs_send and n >= 2 else blocks[6], sem.at[n, 0])
                departed(blocks[24], sem.at[n, 1])

    def gain_of(layer):
        chosen = lax.broadcasted_iota(jnp.int32, gains.shape, 0) == layer
        return jnp.sum(jnp.where(chosen, wide(gains[...]), 0.0), axis=0, keepdims=True)

    for copy in small:
        copy.wait()
    gain, far_gain = gain_of(s), gain_of(far)
    steps = {
        "far0": lambda: far_ready(0),
        "far1": lambda: far_ready(1),
        "far2": far_rest,
        "nD0": lambda: gather_inner(D0),
        "nD1": begin_far,
        "nG0": lambda: begin(GA, with_far(cotangent[0, 0], 2)),
        "nN1": lambda: begin(NB, with_far(saved[1, 0, 0], 3)),
        "hD0": lambda: hidden_near(D0),
        "hD1": lambda: hidden_near(D1),
        "nF1": begin_later_forward,
        "nG1": begin_later_grads,
        "w1a": lambda: weight_grad(3, (GA, GB), 0, grad_down),
        "w1b": lambda: weight_grad(3, (GA, GB), 1, grad_down),
        "w0a": lambda: weight_grad(0, (D0, D1, NB), 0, grad_up),
        "w0b": lambda: weight_grad(0, (D0, D1, NB), 1, grad_up),
        "end": end,
    }
    for a, name in enumerate(("D0", "D1", "G0", "N1", "F1", "G1")):
        steps["ir" + name] = functools.partial(gather_pass, a)
        steps["out" + name] = functools.partial(gather_outer, a)
        steps["rel" + name] = functools.partial(gather_relay, a)
    for period in range(2):
        k = str(period)
        steps["hF" + k] = functools.partial(hidden_forward, period)
        steps["hB" + k] = functools.partial(hidden_backward, period)
        steps["gB" + k] = functools.partial(slope, period)
        steps["keepB" + k] = functools.partial(keep_slope, period)
        steps["finF" + k] = functools.partial(finish_forward, period)
        steps["finB" + k] = functools.partial(finish_backward, period)
        for h in range(2):
            steps[f"pF{k}h{h}"] = lambda p=2 * period, h=h: onto_features(p, h, active[...], weights_of(1))
            steps[f"pB{k}h{h}"] = lambda p=2 * period + 1, h=h: onto_features(
                p, h, slopes[p // 2], weights_of(0)
            )
        for n, name in enumerate("FB"):
            steps["rsr" + name + k] = functools.partial(scatter_relay, 2 * period + n)
            steps["rsi" + name + k] = functools.partial(scatter_inner, 2 * period + n)
    for n, value in enumerate((states_in[1, 0], saved[0, 1, 0], cotangent[1, 0], saved[1, 1, 0])):
        far_out[n] = folded(value)
    begin_near(D0, wide(states_in[0, 0]), wide(saved[0, 0, 0]))
    pl.semaphore_wait(barrier, len(partners))
    for name in ORDER:
        steps[name]()


def write_out(*refs):
    sems = refs[-1]
    copies = [pltpu.make_async_copy(refs[n], refs[4 + n], sems.at[n]) for n in range(4)]
    for copy in copies:
        copy.start()
    for copy in copies:
        copy.wait()


def body(states_in, entering, saved, cotangent, cot_entering, gains, up_rows, down_rows):
    units, features = up_rows.shape[2:]
    width = features // 2
    dma, vmem = pltpu.SemaphoreType.DMA, pltpu.VMEM
    in_vmem = pl.BlockSpec(memory_space=pltpu.VMEM)
    anywhere = pl.BlockSpec(memory_space=pl.ANY)
    grid_rows = (RING, RING, 16, width)
    shapes = (saved.shape, saved.shape, (1, units, features), (1, units, features))
    results = pl.pallas_call(
        kernel,
        out_shape=tuple(vmem(shape, BF16) for shape in shapes),
        in_specs=[anywhere] * 8,
        out_specs=(in_vmem,) * 4,
        scratch_shapes=[
            vmem((2, units, width), BF16),
            vmem((2, units, width), BF16),
            vmem((6, 2) + grid_rows, BF16),
            vmem((4, 2) + grid_rows, BF16),
            vmem((4, 2) + grid_rows[1:], BF16),
            vmem((4, 2) + grid_rows[1:], BF16),
            vmem((4, 2) + grid_rows[1:], BF16),
            vmem((4, 2) + grid_rows[1:], BF16),
            vmem((4, 2, 3, 16, width), BF16),
            vmem((2, 2, 2, RING, 16, width // 2), BF16),
            vmem((2, 2, 7, 16, width // 2), BF16),
            vmem((6, 16, features), F32),
            vmem((6, 16, width), BF16),
            vmem((6, 16, width), BF16),
            vmem((2, 16, features), BF16),
            vmem((2, 16, features), BF16),
            vmem((16, features), F32),
            vmem((2, 16, width), BF16),
            vmem((2, 16, width), BF16),
            vmem((2, 256, units), BF16),
            vmem((2, 256, units), F32),
            vmem((256, units), BF16),
            vmem((5, units, 256), BF16),
            vmem((2, 16, 2, 8, units), F32),
            vmem(states_in.shape, BF16),
            vmem(entering.shape, BF16),
            vmem(saved.shape, BF16),
            vmem(cotangent.shape, BF16),
            vmem(cot_entering.shape, BF16),
            vmem(gains.shape, BF16),
            dma((4,)),
            dma((6,)),
            dma((6, 2)),
            dma((6, 4)),
            dma((4, 2)),
            dma((4, 3)),
            dma((1,)),
            dma((6,)),
            dma((2,)),
            dma((2,)),
            dma((1,)),
            dma((2,)),
        ],
        compiler_params=pltpu.CompilerParams(
            collective_id=0, has_side_effects=True, vmem_limit_bytes=48 * 2**20
        ),
        cost_estimate=pl.CostEstimate(flops=15 * 10**9, bytes_accessed=17 * 10**6, transcendentals=0),
    )(states_in, entering, saved, cotangent, cot_entering, gains, up_rows, down_rows)
    return pl.pallas_call(
        write_out,
        out_shape=tuple(jax.ShapeDtypeStruct(shape, BF16) for shape in shapes),
        in_specs=[in_vmem] * 4,
        out_specs=(anywhere,) * 4,
        scratch_shapes=[dma((4,))],
        compiler_params=pltpu.CompilerParams(vmem_limit_bytes=4 * 2**20),
    )(*results)


def solution(mesh):
    group = ("dp", "tensor")
    placed = (
        P(None, "section", group, None),
        P(None, None, group, None),
        P(None, None, "section", group, None),
        P(None, "section", group, None),
        P(None, None, group, None),
        P(),
        P("section", None, group, None),
        P("section", None, group, None),
    )
    return jax.shard_map(
        body,
        mesh=mesh,
        in_specs=placed,
        out_specs=(
            P(None, None, "section", group, None),
            P(None, None, "section", group, None),
            P("section", group, None),
            P("section", group, None),
        ),
        check_vma=False,
    )
```
